128 devices in a mesh: dp: 4 (over x), tensor: 32 (over y, z, core).
Axes of the slice: x: 4, y: 4, z: 4, core: 2. Of those that a mesh axis runs over, the one named last changes fastest.
Arguments:
- activations: bfloat16 [1024, 8192], P('dp', 'tensor'), may hold values from -6 to 6
- gate_weight: bfloat16 [8192, 28672], P('dp', 'tensor'), may hold values from -0.0625 to 0.0625
- up_weight: bfloat16 [8192, 28672], P('dp', 'tensor'), may hold values from -0.0625 to 0.0625
- group_mix: float32 [7, 7], replicated, may hold values from -2 to 2
- down_weight: bfloat16 [28672, 8192], P('tensor'), may hold values from -0.03125 to 0.03125
Outputs:
- ffn_out: bfloat16 [1024, 8192], P('dp', 'tensor')
The draws below stay inside these ranges and needn't reach their ends.
All inputs are finite; a program needn't handle non-finite values.
Results may differ from the reference program's by a relative error of at most 0.0065.
Values may be sent and summed in bfloat16 or wider, within the bound.
A program may use at most 128 MiB of HBM per device.

```python
import math
import jax
import jax.numpy as jnp
from jax import lax

D = 8192
FF = 28672
GROUP = 7
HAD = 4096
TOKENS = 1024


def shard_levels(key, dims, split, least, largest):
    factor_of = 1.0
    for axis_at, shards_of in split:
        steps = jax.random.uniform(jax.random.fold_in(jax.random.fold_in(key, 6), axis_at), (shards_of,), jnp.float32, least / len(split), largest / len(split))
        factor_of = factor_of * jnp.repeat(jnp.exp(steps), dims[axis_at] // shards_of).reshape((-1,) + (1,) * (len(dims) - 1 - axis_at))
    return factor_of


def scatter_about(own_key, dims, width, most, cuts=(), kind=jnp.bfloat16):
    factor_of = shard_levels(own_key, dims, cuts, -0.22, 0.18) if cuts else 1.0
    entries = jax.random.normal(own_key, dims, jnp.float32) * width * factor_of
    return jnp.minimum(jnp.maximum(entries, -most), most).astype(kind)


def setup_inputs(seed: int = 0) -> dict:
    seeds = jax.random.split(jax.random.key(seed), 6)
    return {
        "activations": scatter_about(seeds[0], (TOKENS, D), 1.0, 6.0, ((0, 4), (1, 32))),
        "gate_weight": scatter_about(seeds[1], (D, FF), D ** -0.5, 0.0625, ((0, 4), (1, 32))),
        "up_weight": scatter_about(seeds[2], (D, FF), D ** -0.5, 0.0625, ((0, 4), (1, 32))),
        "group_mix": scatter_about(seeds[3], (GROUP, GROUP), GROUP ** -0.5, 2.0, (), jnp.float32),
        "down_weight": scatter_about(seeds[4], (FF, D), FF ** -0.5, 0.03125, ((0, 32),)),
    }


def walsh_rows(grouped):
    half_span = 1
    while half_span < HAD:
        shaped = grouped.reshape(TOKENS, HAD // (2 * half_span), 2, half_span, GROUP)
        first_part = shaped[:, :, 0]
        second_part = shaped[:, :, 1]
        grouped = jnp.stack([first_part + second_part, first_part - second_part], axis=2).reshape(TOKENS, HAD, GROUP)
        half_span = half_span * 2
    return grouped

def reference(activations, gate_weight, up_weight, group_mix, down_weight):
    gate_sum = jnp.dot(activations, gate_weight, preferred_element_type=jnp.float32)
    up_sum = jnp.dot(activations, up_weight, preferred_element_type=jnp.float32)
    hidden = (jax.nn.silu(gate_sum) * up_sum).astype(jnp.bfloat16)
    grouped = hidden.astype(jnp.float32).reshape(TOKENS, HAD, GROUP)
    grouped = jnp.einsum('tbc,ac->tba', grouped, group_mix, precision=lax.Precision.HIGHEST)
    rotated = (walsh_rows(grouped) * (1.0 / math.sqrt(HAD))).reshape(TOKENS, FF).astype(jnp.bfloat16)
    return jnp.dot(rotated, down_weight, preferred_element_type=jnp.float32).astype(jnp.bfloat16)
```

```python
import jax
import jax.numpy as jnp
from jax import lax
from jax.experimental import pallas as pl
from jax.experimental.pallas import tpu as pltpu
from jax.sharding import PartitionSpec as P

MESH = pl.DeviceIdType.MESH
BF = jnp.bfloat16
F32 = jnp.float32

CHUNKS = 2
RB = 256 // CHUNKS
Q = RB // 4
HB = RB // 2
TILES = 7
SPAN = 896
GROUPS = 8


def wait_for(ref, sem):
    pltpu.make_async_copy(ref, ref, sem).wait()


def pack(pairs_of):
    out = []
    for i in range(0, GROUPS, 2):
        first = pairs_of[i]
        second = pairs_of[i + 1] if i + 1 < TILES else jnp.zeros_like(first)
        out.append(jnp.concatenate([first, second], axis=1).astype(BF))
    return jnp.concatenate(out, axis=1)


def unpack(packed):
    out = []
    for i in range(0, GROUPS, 2):
        pair = packed[:, i * 8 : i * 8 + 16, :].astype(F32)
        out.append(pair[:, :8, :].reshape(16 * 8, 128).astype(BF))
        if i + 1 < TILES:
            out.append(pair[:, 8:, :].reshape(16 * 8, 128).astype(BF))
    return jnp.concatenate(out, axis=1)


def kernel(
    act, gate, up, gm, down, out,
    wv, dv, af, pacc, own, nb, xo, xn, ro, rn,
    mhi, mlo, hs, hr, rs, rr, rot, ds, dk, dr, es, f1, g2, f2,
    w_sem, d_sem, a1_s, a1_r, ag_s, ag_r, xo_s, xo_r, xn_s, xn_r,
    h_s, h_r, ds_s, ds_r, e_s, e_r,
):
    x = lax.axis_index("dp")
    t = lax.axis_index("tensor")
    y, z, c = t // 8, (t // 2) % 4, t % 2
    p = t // 2
    sib = 1 - c
    xp, xm = (x + 1) % 4, (x + 3) % 4
    col = pl.multiple_of(c * 1024 + z * 256, 256)
    ccol = pl.multiple_of(c * 1024, 1024)

    def at(x_, y_, z_, c_):
        return (x_, y_ * 8 + z_ * 2 + c_)

    def send(src, dst, ss, rs_, dev):
        pltpu.make_async_remote_copy(
            src_ref=src, dst_ref=dst, send_sem=ss, recv_sem=rs_, device_id=dev, device_id_type=MESH
        ).start()

    for j in range(TILES):
        for cc in range(2):
            cols = pl.ds(j * 128, 128)
            pltpu.make_async_copy(gate.at[:, cc, :, cols], wv.at[j, cc, :, :, pl.ds(0, 128)], w_sem).start()
            pltpu.make_async_copy(up.at[:, cc, :, cols], wv.at[j, cc, :, :, pl.ds(128, 128)], w_sem).start()
    for j in range(16):
        pltpu.make_async_copy(down.at[:, pl.ds(j * 512, 512)], dv.at[j], d_sem).start()

    bar = pltpu.get_barrier_semaphore()

    def greet(dev):
        pl.semaphore_signal(bar, inc=1, device_id=dev, device_id_type=MESH)

    same = x == y
    greet((xp, t))
    greet((xm, t))
    greet(at(x, y, z, sib))
    for k in range(4):
        @pl.when(jnp.logical_not(jnp.logical_and(same, y == k)))
        def _():
            greet(at(y, k, z, c))

        @pl.when(jnp.logical_not(jnp.logical_and(same, x == k)))
        def _():
            greet(at(k, x, z, c))

    def greet_plane(i, carry):
        q = (p + i) % 16
        greet((x, q * 2 + c))
        return carry

    lax.fori_loop(1, 16, greet_plane, 0)
    pl.semaphore_wait(bar, jnp.where(same, 24, 26))

    def act_first(r):
        for k in range(4):
            src = act.at[pl.ds(r * RB + k * Q, Q), :]
            dst = af.at[r, x, k, :, pl.ds(col, 256)]
            here = jnp.logical_and(same, y == k)

            @pl.when(here)
            def _():
                pltpu.make_async_copy(src, dst, a1_r.at[r]).start()

            @pl.when(jnp.logical_not(here))
            def _():
                send(src, dst, a1_s.at[r, k], a1_r.at[r], at(y, k, z, c))

    def act_first_done(r):
        wait_for(af.at[r, :, 0, :, pl.ds(0, 256)], a1_r.at[r])

    def act_a(r):
        for i in range(1, 4):
            piece = af.at[r, pl.ds(0, 2), y, :, pl.ds(col, 256)]
            send(piece, piece, ag_s.at[r, 0], ag_r.at[r, 0], at(x, (y + i) % 4, z, c))
            piece = af.at[r, pl.ds(2, 2), y, :, pl.ds(col, 256)]
            send(piece, piece, ag_s.at[r, 1], ag_r.at[r, 1], at(x, y, (z + i) % 4, c))

    def act_b(r):
        wait_for(af.at[r, pl.ds(0, 2), pl.ds(0, 3), :, pl.ds(0, 256)], ag_r.at[r, 0])
        for i in range(1, 4):
            piece = af.at[r, pl.ds(0, 2), :, :, pl.ds(col, 256)]
            send(piece, piece, ag_s.at[r, 2], ag_r.at[r, 2], at(x, y, (z + i) % 4, c))
        wait_for(af.at[r, pl.ds(2, 2), 0, :, pl.ds(0, 768)], ag_r.at[r, 1])
        for i in range(1, 4):
            piece = af.at[r, pl.ds(2, 2), y, :, pl.ds(ccol, 1024)]
            send(piece, piece, ag_s.at[r, 3], ag_r.at[r, 3], at(x, (y + i) % 4, z, c))

    def act_sib(r):
        wait_for(af.at[r, pl.ds(0, 2), :, :, pl.ds(0, 768)], ag_r.at[r, 2])
        wait_for(af.at[r, pl.ds(2, 2), pl.ds(0, 3), :, pl.ds(0, 1024)], ag_r.at[r, 3])
        piece = af.at[r, :, :, :, pl.ds(ccol, 1024)]
        send(piece, piece, ag_s.at[r, 4], ag_r.at[r, 4], at(x, y, z, sib))

    def act_done(r):
        wait_for(af.at[r, :, :, :, pl.ds(0, 1024)], ag_r.at[r, 4])

    def act_sent(r):
        for k in range(4):
            @pl.when(jnp.logical_not(jnp.logical_and(same, y == k)))
            def _():
                wait_for(af.at[r, 0, 0, :, pl.ds(0, 256)], a1_s.at[r, k])
        wait_for(af.at[r, pl.ds(0, 2), pl.ds(0, 3), :, pl.ds(0, 256)], ag_s.at[r, 0])
        wait_for(af.at[r, pl.ds(2, 2), 0, :, pl.ds(0, 768)], ag_s.at[r, 1])
        wait_for(af.at[r, pl.ds(0, 2), :, :, pl.ds(0, 768)], ag_s.at[r, 2])
        wait_for(af.at[r, pl.ds(2, 2), pl.ds(0, 3), :, pl.ds(0, 1024)], ag_s.at[r, 3])
        wait_for(af.at[r, :, :, :, pl.ds(0, 1024)], ag_s.at[r, 4])

    def multiply(r):
        def step(j, carry):
            w = wv[j].reshape(2048, 256)
            a = af[r].reshape(4 * RB, 2048)
            pacc[...] = jnp.dot(a, w, preferred_element_type=F32).reshape(4, RB, 256)
            far = pacc[(x + 2) % 4].astype(BF)
            xo[r, j, 0] = far[:HB]
            xo[r, j, 1] = far[HB:]
            send(xo.at[r, j, 0], ro.at[r, 0, j], xo_s.at[r], xo_r.at[r, 0, j], (xp, t))
            send(xo.at[r, j, 1], ro.at[r, 1, j], xo_s.at[r], xo_r.at[r, 1, j], (xm, t))
            nxt = pacc[xp]
            nb[0, j] = nxt[:HB]
            xn[r, 0, j, 1] = nxt[HB:].astype(BF)
            send(xn.at[r, 0, j, 1], rn.at[r, 0, j, 1], xn_s.at[r], xn_r.at[r, 0], (xp, t))
            prv = pacc[xm]
            nb[1, j] = prv[HB:]
            xn[r, 1, j, 0] = prv[:HB].astype(BF)
            send(xn.at[r, 1, j, 0], rn.at[r, 1, j, 0], xn_s.at[r], xn_r.at[r, 1], (xm, t))
            own[r, j] = pacc[x]
            return carry

        lax.fori_loop(0, TILES, step, 0)

    def relay(r):
        def step(j, carry):
            wait_for(ro.at[r, 0, j], xo_r.at[r, 0, j])
            xn[r, 0, j, 0] = (nb[0, j] + ro[r, 0, j].astype(F32)).astype(BF)
            send(xn.at[r, 0, j, 0], rn.at[r, 0, j, 0], xn_s.at[r], xn_r.at[r, 0], (xp, t))
            wait_for(ro.at[r, 1, j], xo_r.at[r, 1, j])
            xn[r, 1, j, 1] = (nb[1, j] + ro[r, 1, j].astype(F32)).astype(BF)
            send(xn.at[r, 1, j, 1], rn.at[r, 1, j, 1], xn_s.at[r], xn_r.at[r, 1], (xm, t))
            return carry

        lax.fori_loop(0, TILES, step, 0)

    def reduce_sent(r):
        wait_for(xo.at[r], xo_s.at[r])
        wait_for(xn.at[r], xn_s.at[r])

    def hide(r):
        wait_for(rn.at[r, 0], xn_r.at[r, 0])
        wait_for(rn.at[r, 1], xn_r.at[r, 1])
        groups = []
        for j in range(TILES):
            s = own[r, j] + rn[r, 0, j].reshape(RB, 256).astype(F32) + rn[r, 1, j].reshape(RB, 256).astype(F32)
            g, u = s[:, :128], s[:, 128:]
            groups.append((g / (1.0 + jnp.exp(-g)) * u).reshape(16, 8, 128))
        hs[r] = pack(groups)
        hr[r, c, p] = hs[r, p]

        def step(i, carry):
            q = (p + i) % 16
            send(hs.at[r, q], hr.at[r, c, p], h_s.at[r, 0], h_r.at[r, 0], (x, q * 2 + c))
            return carry

        lax.fori_loop(1, 16, step, 0)

    def hide_sib(r):
        wait_for(hs.at[r, pl.ds(0, 15)], h_r.at[r, 0])
        send(hr.at[r, c], hr.at[r, c], h_s.at[r, 1], h_r.at[r, 1], at(x, y, z, sib))

    def mix(r):
        wait_for(hs.at[r], h_r.at[r, 1])
        both = jnp.concatenate([unpack(hr[r, 0]), unpack(hr[r, 1])], axis=0)
        mixed = jnp.dot(both, mhi[...], preferred_element_type=F32)
        mixed = mixed + jnp.dot(both, mlo[...], preferred_element_type=F32)
        sign = jnp.where(c == 0, 1.0, -1.0).astype(F32)
        s = mixed[:128] + sign * mixed[128:]
        parts = [s[8 * i : 8 * i + 8] for i in range(16)]
        half = 1
        while half < 16:
            for i in range(16):
                if i & half == 0:
                    a, b = parts[i], parts[i + half]
                    parts[i], parts[i + half] = a + b, a - b
            half *= 2
        for i in range(16):
            rs[r, i] = pack([parts[i][None, :, 128 * g : 128 * g + 128] for g in range(TILES)])[0]
        rr[r, p] = rs[r, p]

        def step(i, carry):
            q = (p + i) % 16
            send(rs.at[r, q], rr.at[r, p], h_s.at[r, 2], h_r.at[r, 2], (x, q * 2 + c))
            return carry

        lax.fori_loop(1, 16, step, 0)

    def mix_sent(r):
        wait_for(hs.at[r, pl.ds(0, 15)], h_s.at[r, 0])
        wait_for(hs.at[r], h_s.at[r, 1])
        wait_for(hs.at[r, pl.ds(0, 15)], h_s.at[r, 2])

    def project(r):
        wait_for(rr.at[r, pl.ds(0, 15)], h_r.at[r, 2])
        rot[...] = unpack(rr[r])

        def step(i, carry):
            d = jnp.dot(rot[...], dv[i], preferred_element_type=F32)
            left, right = d[:, :256], d[:, 256:]
            dk[i] = jnp.where(c == 0, left, right)
            ds[r, i] = jnp.where(c == 0, right, left).astype(BF)
            send(ds.at[r, i], dr.at[r, i], ds_s.at[r], ds_r.at[r, i], at(x, y, z, sib))
            return carry

        lax.fori_loop(0, 16, step, 0)

    def spread(r):
        def step(i, carry):
            wait_for(dr.at[r, i], ds_r.at[r, i])
            e = (dk[i] + dr[r, i].astype(F32)).astype(BF)
            es[r, 0, i // 4, i % 4] = e[:HB]
            es[r, 1, i // 4, i % 4] = e[HB:]
            return carry

        lax.fori_loop(0, 16, step, 0)
        for i in range(1, 4):
            zz, yy = (z + i) % 4, (y + i) % 4
            send(es.at[r, 0, :, zz], f1.at[r, 0, i - 1], e_s.at[r, 0], e_r.at[r, 0], at(x, y, zz, c))
            send(es.at[r, 1, yy], f1.at[r, 1, i - 1], e_s.at[r, 1], e_r.at[r, 1], at(x, yy, z, c))

    def gather_one(r):
        wait_for(f1.at[r, 0], e_r.at[r, 0])
        g0 = es[r, 0, :, z].astype(F32)
        for i in range(3):
            g0 = g0 + f1[r, 0, i].astype(F32)
        g2[r, 0] = g0.astype(BF)
        for i in range(1, 4):
            yy = (y + i) % 4
            send(g2.at[r, 0, yy], f2.at[r, 0, i - 1], e_s.at[r, 2], e_r.at[r, 2], at(x, yy, z, c))
        wait_for(f1.at[r, 1], e_r.at[r, 1])
        g1 = es[r, 1, y].astype(F32)
        for i in range(3):
            g1 = g1 + f1[r, 1, i].astype(F32)
        g2[r, 1] = g1.astype(BF)
        for i in range(1, 4):
            zz = (z + i) % 4
            send(g2.at[r, 1, zz], f2.at[r, 1, i - 1], e_s.at[r, 3], e_r.at[r, 3], at(x, y, zz, c))

    def finish(r):
        for h, own_block in ((0, y), (1, z)):
            wait_for(f2.at[r, h], e_r.at[r, 2 + h])
            total = g2[r, h, own_block].astype(F32)
            for i in range(3):
                total = total + f2[r, h, i].astype(F32)
            out[pl.ds(r * RB + h * HB, HB), :] = total.astype(BF)

    def project_sent(r):
        wait_for(ds.at[r], ds_s.at[r])
        wait_for(f1.at[r, 0], e_s.at[r, 0])
        wait_for(f1.at[r, 1], e_s.at[r, 1])
        wait_for(f2.at[r, 0], e_s.at[r, 2])
        wait_for(f2.at[r, 1], e_s.at[r, 3])

    act_first(0)
    act_first(1)

    def build(i, carry):
        f_in = i * 128 + lax.broadcasted_iota(jnp.int32, (128, SPAN), 0)
        f_out = lax.broadcasted_iota(jnp.int32, (128, SPAN), 1)
        b_in, b_out = (f_in * 9363) >> 16, (f_out * 9363) >> 16
        a_in, a_out = f_in - 7 * b_in, f_out - 7 * b_out
        v = b_in & b_out
        v = v ^ (v >> 4)
        v = v ^ (v >> 2)
        v = v ^ (v >> 1)
        sign = (1 - 2 * (v & 1)).astype(F32)
        value = jnp.zeros((128, SPAN), F32)
        a_row = a_out[:8]
        for k in range(7):
            row = jnp.zeros((8, SPAN), F32)
            for m in range(7):
                row = jnp.where(a_row == m, gm[m, k], row)
            value = jnp.where(a_in == k, row[:1], value)
        value = value * sign * (1.0 / 64.0)
        hi = value.astype(BF)
        rows = pl.ds(pl.multiple_of(i * 128, 128), 128)
        mhi[rows, :] = hi
        mlo[rows, :] = (value - hi.astype(F32)).astype(BF)
        return carry

    lax.fori_loop(0, TILES, build, 0)

    act_first_done(0)
    act_a(0)
    act_first_done(1)
    act_a(1)
    act_b(0)
    act_b(1)
    act_sib(0)
    wait_for(wv, w_sem)
    act_done(0)
    multiply(0)
    act_sib(1)
    relay(0)
    act_done(1)
    multiply(1)
    hide(0)
    relay(1)
    hide_sib(0)
    mix(0)
    wait_for(dv, d_sem)
    project(0)
    spread(0)
    gather_one(0)
    hide(1)
    hide_sib(1)
    finish(0)
    mix(1)
    project(1)
    spread(1)
    gather_one(1)
    finish(1)
    for r in range(CHUNKS):
        act_sent(r)
        reduce_sent(r)
        mix_sent(r)
        project_sent(r)


def local(activations, gate_weight, up_weight, group_mix, down_weight):
    any_space = pl.BlockSpec(memory_space=pl.ANY)
    dma = pltpu.SemaphoreType.DMA
    vm = pltpu.VMEM
    r = CHUNKS
    scratch = [
        vm((TILES, 2, 4, 256, 256), BF),
        vm((16, SPAN, 512), BF),
        vm((r, 4, 4, Q, 2048), BF),
        vm((4, RB, 256), F32),
        vm((r, TILES, RB, 256), F32),
        vm((2, TILES, HB, 256), F32),
        vm((r, TILES, 2, HB, 256), BF),
        vm((r, 2, TILES, 2, HB, 256), BF),
        vm((r, 2, TILES, HB, 256), BF),
        vm((r, 2, TILES, 2, HB, 256), BF),
        vm((SPAN, SPAN), BF),
        vm((SPAN, SPAN), BF),
        vm((r, 16, 64, 128), BF),
        vm((r, 2, 16, 64, 128), BF),
        vm((r, 16, 64, 128), BF),
        vm((r, 16, 64, 128), BF),
        vm((RB, SPAN), BF),
        vm((r, 16, RB, 256), BF),
        vm((16, RB, 256), F32),
        vm((r, 16, RB, 256), BF),
        vm((r, 2, 4, 4, HB, 256), BF),
        vm((r, 2, 3, 4, HB, 256), BF),
        vm((r, 2, 4, HB, 256), BF),
        vm((r, 2, 3, HB, 256), BF),
        dma(()), dma(()),
        dma((r, 4)), dma((r,)),
        dma((r, 5)), dma((r, 5)),
        dma((r,)), dma((r, 2, TILES)),
        dma((r,)), dma((r, 2)),
        dma((r, 3)), dma((r, 3)),
        dma((r,)), dma((r, 16)),
        dma((r, 4)), dma((r, 4)),
    ]
    return pl.pallas_call(
        kernel,
        out_shape=jax.ShapeDtypeStruct((256, 256), BF),
        in_specs=[any_space, any_space, any_space, pl.BlockSpec(memory_space=pltpu.SMEM), any_space],
        out_specs=pl.BlockSpec(memory_space=pltpu.VMEM),
        scratch_shapes=scratch,
        compiler_params=pltpu.CompilerParams(
            collective_id=0, has_side_effects=True, vmem_limit_bytes=60 * 1024 * 1024
        ),
        cost_estimate=pl.CostEstimate(flops=12_000_000_000, bytes_accessed=24_000_000, transcendentals=230_000),
        name="ffn",
    )(
        activations,
        gate_weight.reshape(4, 2, 256, SPAN),
        up_weight.reshape(4, 2, 256, SPAN),
        group_mix,
        down_weight,
    )


def solution(mesh):
    return jax.shard_map(
        local,
        mesh=mesh,
        in_specs=(P("dp", "tensor"), P("dp", "tensor"), P("dp", "tensor"), P(), P("tensor", None)),
        out_specs=P("dp", "tensor"),
        check_vma=False,
    )
```

```python
import jax
import jax.numpy as jnp
from jax import lax
from jax.experimental import pallas as pl
from jax.experimental.pallas import tpu as pltpu
from jax.sharding import PartitionSpec as P

MESH = pl.DeviceIdType.MESH
BF = jnp.bfloat16
F32 = jnp.float32

CHUNKS = 4
RB = 256 // CHUNKS
PARTS = 2
PER = CHUNKS // PARTS
RT = 256 // PARTS
HT = RT // 2
Q = RB // 4
HB = RB // 2
TILES = 7
SPAN = 896
LAG = 4
GROUPS = 8


def wait_for(ref, sem):
    pltpu.make_async_copy(ref, ref, sem).wait()


def pack(pairs_of):
    out = []
    for i in range(0, GROUPS, 2):
        first = pairs_of[i]
        second = pairs_of[i + 1] if i + 1 < TILES else jnp.zeros_like(first)
        out.append(jnp.concatenate([first, second], axis=1).astype(BF))
    return jnp.concatenate(out, axis=1)


def unpack(packed):
    out = []
    for i in range(0, GROUPS, 2):
        pair = packed[:, i * 8 : i * 8 + 16, :].astype(F32)
        out.append(pair[:, :8, :].reshape(16 * 8, 128).astype(BF))
        if i + 1 < TILES:
            out.append(pair[:, 8:, :].reshape(16 * 8, 128).astype(BF))
    return jnp.concatenate(out, axis=1)


def kernel(
    act, gate, up, gm, down, out,
    wv, dv, af, pacc, own, nb, xo, xn, ro, rn,
    mhi, mlo, hs, hr, rs, rr, rot, ds, dk, dr, es, f1, g2, f2,
    w_sem, d_sem, a1_s, a1_r, ag_s, ag_r, xo_s, xo_r, xn_s, xn_r,
    h_s, h_r, ds_s, ds_r, e_s, e_r,
):
    x = lax.axis_index("dp")
    t = lax.axis_index("tensor")
    y, z, c = t // 8, (t // 2) % 4, t % 2
    p = t // 2
    sib = 1 - c
    xp, xm = (x + 1) % 4, (x + 3) % 4
    col = pl.multiple_of(c * 1024 + z * 256, 256)
    ccol = pl.multiple_of(c * 1024, 1024)

    def at(x_, y_, z_, c_):
        return (x_, y_ * 8 + z_ * 2 + c_)

    def send(src, dst, ss, rs_, dev):
        pltpu.make_async_remote_copy(
            src_ref=src, dst_ref=dst, send_sem=ss, recv_sem=rs_, device_id=dev, device_id_type=MESH
        ).start()

    for j in range(TILES):
        for cc in range(2):
            cols = pl.ds(j * 128, 128)
            pltpu.make_async_copy(gate.at[:, cc, :, cols], wv.at[j, cc, :, :, pl.ds(0, 128)], w_sem).start()
            pltpu.make_async_copy(up.at[:, cc, :, cols], wv.at[j, cc, :, :, pl.ds(128, 128)], w_sem).start()
    bar = pltpu.get_barrier_semaphore()

    def greet(dev):
        pl.semaphore_signal(bar, inc=1, device_id=dev, device_id_type=MESH)

    same = x == y
    greet((xp, t))
    greet((xm, t))
    greet(at(x, y, z, sib))
    for k in range(4):
        @pl.when(jnp.logical_not(jnp.logical_and(same, y == k)))
        def _():
            greet(at(y, k, z, c))

        @pl.when(jnp.logical_not(jnp.logical_and(same, x == k)))
        def _():
            greet(at(k, x, z, c))

    for k in range(1, 4):
        greet(at(x, (y + k) % 4, z, c))
        greet(at(x, y, (z + k) % 4, c))
    pl.semaphore_wait(bar, jnp.where(same, 15, 17))

    def down_start():
        for j in range(16):
            pltpu.make_async_copy(down.at[:, pl.ds(j * 512, 512)], dv.at[j], d_sem).start()

    def act_first(r):
        for k in range(4):
            src = act.at[pl.ds(r * RB + k * Q, Q), :]
            dst = af.at[r, x, k, :, pl.ds(col, 256)]
            here = jnp.logical_and(same, y == k)

            @pl.when(here)
            def _():
                pltpu.make_async_copy(src, dst, a1_r.at[r]).start()

            @pl.when(jnp.logical_not(here))
            def _():
                send(src, dst, a1_s.at[r, k], a1_r.at[r], at(y, k, z, c))

    def act_first_done(r):
        wait_for(af.at[r, :, 0, :, pl.ds(0, 256)], a1_r.at[r])

    def act_a(r):
        for i in range(1, 4):
            piece = af.at[r, pl.ds(0, 2), y, :, pl.ds(col, 256)]
            send(piece, piece, ag_s.at[r, 0], ag_r.at[r, 0], at(x, (y + i) % 4, z, c))
            piece = af.at[r, pl.ds(2, 2), y, :, pl.ds(col, 256)]
            send(piece, piece, ag_s.at[r, 1], ag_r.at[r, 1], at(x, y, (z + i) % 4, c))

    def act_b(r):
        wait_for(af.at[r, pl.ds(0, 2), pl.ds(0, 3), :, pl.ds(0, 256)], ag_r.at[r, 0])
        for i in range(1, 4):
            piece = af.at[r, pl.ds(0, 2), :, :, pl.ds(col, 256)]
            send(piece, piece, ag_s.at[r, 2], ag_r.at[r, 2], at(x, y, (z + i) % 4, c))
        wait_for(af.at[r, pl.ds(2, 2), 0, :, pl.ds(0, 768)], ag_r.at[r, 1])
        for i in range(1, 4):
            piece = af.at[r, pl.ds(2, 2), y, :, pl.ds(ccol, 1024)]
            send(piece, piece, ag_s.at[r, 3], ag_r.at[r, 3], at(x, (y + i) % 4, z, c))

    def act_sib(r):
        wait_for(af.at[r, pl.ds(0, 2), :, :, pl.ds(0, 768)], ag_r.at[r, 2])
        wait_for(af.at[r, pl.ds(2, 2), pl.ds(0, 3), :, pl.ds(0, 1024)], ag_r.at[r, 3])
        piece = af.at[r, :, :, :, pl.ds(ccol, 1024)]
        send(piece, piece, ag_s.at[r, 4], ag_r.at[r, 4], at(x, y, z, sib))

    def act_done(r):
        wait_for(af.at[r, :, :, :, pl.ds(0, 1024)], ag_r.at[r, 4])

    def act_sent(r):
        for k in range(4):
            @pl.when(jnp.logical_not(jnp.logical_and(same, y == k)))
            def _():
                wait_for(af.at[r, 0, 0, :, pl.ds(0, 256)], a1_s.at[r, k])
        wait_for(af.at[r, pl.ds(0, 2), pl.ds(0, 3), :, pl.ds(0, 256)], ag_s.at[r, 0])
        wait_for(af.at[r, pl.ds(2, 2), 0, :, pl.ds(0, 768)], ag_s.at[r, 1])
        wait_for(af.at[r, pl.ds(0, 2), :, :, pl.ds(0, 768)], ag_s.at[r, 2])
        wait_for(af.at[r, pl.ds(2, 2), pl.ds(0, 3), :, pl.ds(0, 1024)], ag_s.at[r, 3])
        wait_for(af.at[r, :, :, :, pl.ds(0, 1024)], ag_s.at[r, 4])

    def multiply(r):
        def step(j, carry):
            w = wv[j].reshape(2048, 256)
            a = af[r].reshape(4 * RB, 2048)
            pacc[...] = jnp.dot(a, w, preferred_element_type=F32).reshape(4, RB, 256)
            far = pacc[(x + 2) % 4].astype(BF)
            xo[r, j, 0] = far[:HB]
            xo[r, j, 1] = far[HB:]
            send(xo.at[r, j, 0], ro.at[r, 0, j], xo_s.at[r], xo_r.at[r, 0, j], (xp, t))
            send(xo.at[r, j, 1], ro.at[r, 1, j], xo_s.at[r], xo_r.at[r, 1, j], (xm, t))
            nxt = pacc[xp]
            nb[r, 0, j] = nxt[:HB]
            xn[r, 0, j, 1] = nxt[HB:].astype(BF)
            send(xn.at[r, 0, j, 1], rn.at[r, 0, j, 1], xn_s.at[r], xn_r.at[r, 0], (xp, t))
            prv = pacc[xm]
            nb[r, 1, j] = prv[HB:]
            xn[r, 1, j, 0] = prv[:HB].astype(BF)
            send(xn.at[r, 1, j, 0], rn.at[r, 1, j, 0], xn_s.at[r], xn_r.at[r, 1], (xm, t))
            own[r, j] = pacc[x]
            return carry

        lax.fori_loop(0, TILES, step, 0)

    def relay(r):
        def step(j, carry):
            wait_for(ro.at[r, 0, j], xo_r.at[r, 0, j])
            xn[r, 0, j, 0] = (nb[r, 0, j] + ro[r, 0, j].astype(F32)).astype(BF)
            send(xn.at[r, 0, j, 0], rn.at[r, 0, j, 0], xn_s.at[r], xn_r.at[r, 0], (xp, t))
            wait_for(ro.at[r, 1, j], xo_r.at[r, 1, j])
            xn[r, 1, j, 1] = (nb[r, 1, j] + ro[r, 1, j].astype(F32)).astype(BF)
            send(xn.at[r, 1, j, 1], rn.at[r, 1, j, 1], xn_s.at[r], xn_r.at[r, 1], (xm, t))
            return carry

        lax.fori_loop(0, TILES, step, 0)

    def reduce_sent(r):
        wait_for(xo.at[r], xo_s.at[r])
        wait_for(xn.at[r], xn_s.at[r])

    def hide(r):
        part, first = r // PER, (r % PER) * (16 // PER)
        wait_for(rn.at[r, 0], xn_r.at[r, 0])
        wait_for(rn.at[r, 1], xn_r.at[r, 1])
        groups = []
        for j in range(TILES):
            s = own[r, j] + rn[r, 0, j].reshape(RB, 256).astype(F32) + rn[r, 1, j].reshape(RB, 256).astype(F32)
            g, u = s[:, :128], s[:, 128:]
            groups.append((g / (1.0 + jnp.exp(-g)) * u).reshape(RB // 8, 8, 128))
        hs[part, first : first + 16 // PER] = pack(groups)

        def step(i, carry):
            q = first + (p + i) % (16 // PER)

            @pl.when(q != p)
            def _():
                send(hs.at[part, q], hr.at[part, c, p], h_s.at[part, 0], h_r.at[part, 0], (x, q * 2 + c))

            @pl.when(q == p)
            def _():
                hr[part, c, p] = hs[part, p]

            return carry

        lax.fori_loop(0, 16 // PER, step, 0)

    def hide_sib(r):
        wait_for(hs.at[r, pl.ds(0, 15)], h_r.at[r, 0])
        send(hr.at[r, c], hr.at[r, c], h_s.at[r, 1], h_r.at[r, 1], at(x, y, z, sib))

    def mix(r):
        wait_for(hs.at[r], h_r.at[r, 1])
        both = jnp.concatenate([unpack(hr[r, 0]), unpack(hr[r, 1])], axis=0)
        mixed = jnp.dot(both, mhi[...], preferred_element_type=F32)
        mixed = mixed + jnp.dot(both, mlo[...], preferred_element_type=F32)
        sign = jnp.where(c == 0, 1.0, -1.0).astype(F32)
        s = mixed[:128] + sign * mixed[128:]
        parts = [s[8 * i : 8 * i + 8] for i in range(16)]
        half = 1
        while half < 16:
            for i in range(16):
                if i & half == 0:
                    a, b = parts[i], parts[i + half]
                    parts[i], parts[i + half] = a + b, a - b
            half *= 2
        for i in range(16):
            rs[r, i] = pack([parts[i][None, :, 128 * g : 128 * g + 128] for g in range(TILES)])[0]
        rr[r, p] = rs[r, p]

        def step(i, carry):
            q = (p + i) % 16
            send(rs.at[r, q], rr.at[r, p], h_s.at[r, 2], h_r.at[r, 2], (x, q * 2 + c))
            return carry

        lax.fori_loop(1, 16, step, 0)

    def mix_sent(r):
        wait_for(hs.at[r, pl.ds(0, 15)], h_s.at[r, 0])
        wait_for(hs.at[r], h_s.at[r, 1])
        wait_for(hs.at[r, pl.ds(0, 15)], h_s.at[r, 2])

    def project(r):
        wait_for(rr.at[r, pl.ds(0, 15)], h_r.at[r, 2])
        rot[...] = unpack(rr[r])

        def spread(i):
            q = (p + 1 + i) % 16
            qy, qz = q // 4, q % 4
            wait_for(dr.at[r, q], ds_r.at[r, q])
            e = (dk[q] + dr[r, q].astype(F32)).astype(BF)
            es[r, 0, qy, qz] = e[:HT]
            es[r, 1, qy, qz] = e[HT:]

            @pl.when(qz != z)
            def _():
                slot = (qz + 3 - z) % 4
                send(es.at[r, 0, qy, qz], f1.at[r, 0, slot, qy], e_s.at[r, 0], e_r.at[r, 0], at(x, y, qz, c))

            @pl.when(qy != y)
            def _():
                slot = (qy + 3 - y) % 4
                send(es.at[r, 1, qy, qz], f1.at[r, 1, slot, qz], e_s.at[r, 1], e_r.at[r, 1], at(x, qy, z, c))

        def step(i, carry):
            q = (p + 1 + i) % 16
            d = jnp.dot(rot[...], dv[q], preferred_element_type=F32)
            left, right = d[:, :256], d[:, 256:]
            dk[q] = jnp.where(c == 0, left, right)
            ds[r, q] = jnp.where(c == 0, right, left).astype(BF)
            send(ds.at[r, q], dr.at[r, q], ds_s.at[r], ds_r.at[r, q], at(x, y, z, sib))

            @pl.when(i >= LAG)
            def _():
                spread(i - LAG)

            return carry

        lax.fori_loop(0, 16, step, 0)

        def last(i, carry):
            spread(i)
            return carry

        lax.fori_loop(16 - LAG, 16, last, 0)

    def gather_one(r):
        wait_for(f1.at[r, 0], e_r.at[r, 0])
        g0 = es[r, 0, :, z].astype(F32)
        for i in range(3):
            g0 = g0 + f1[r, 0, i].astype(F32)
        g2[r, 0] = g0.astype(BF)
        for i in range(1, 4):
            yy = (y + i) % 4
            send(g2.at[r, 0, yy], f2.at[r, 0, i - 1], e_s.at[r, 2], e_r.at[r, 2], at(x, yy, z, c))
        wait_for(f1.at[r, 1], e_r.at[r, 1])
        g1 = es[r, 1, y].astype(F32)
        for i in range(3):
            g1 = g1 + f1[r, 1, i].astype(F32)
        g2[r, 1] = g1.astype(BF)
        for i in range(1, 4):
            zz = (z + i) % 4
            send(g2.at[r, 1, zz], f2.at[r, 1, i - 1], e_s.at[r, 3], e_r.at[r, 3], at(x, y, zz, c))

    def finish(r):
        for h, own_block in ((0, y), (1, z)):
            wait_for(f2.at[r, h], e_r.at[r, 2 + h])
            total = g2[r, h, own_block].astype(F32)
            for i in range(3):
                total = total + f2[r, h, i].astype(F32)
            out[pl.ds(r * RT + h * HT, HT), :] = total.astype(BF)

    def project_sent(r):
        wait_for(ds.at[r], ds_s.at[r])
        wait_for(f1.at[r, 0], e_s.at[r, 0])
        wait_for(f1.at[r, 1], e_s.at[r, 1])
        wait_for(f2.at[r, 0], e_s.at[r, 2])
        wait_for(f2.at[r, 1], e_s.at[r, 3])

    for r in range(CHUNKS):
        act_first(r)

    def build(i, carry):
        f_in = i * 128 + lax.broadcasted_iota(jnp.int32, (128, SPAN), 0)
        f_out = lax.broadcasted_iota(jnp.int32, (128, SPAN), 1)
        b_in, b_out = (f_in * 9363) >> 16, (f_out * 9363) >> 16
        a_in, a_out = f_in - 7 * b_in, f_out - 7 * b_out
        v = b_in & b_out
        v = v ^ (v >> 4)
        v = v ^ (v >> 2)
        v = v ^ (v >> 1)
        sign = (1 - 2 * (v & 1)).astype(F32)
        value = jnp.zeros((128, SPAN), F32)
        a_row = a_out[:8]
        for k in range(7):
            row = jnp.zeros((8, SPAN), F32)
            for m in range(7):
                row = jnp.where(a_row == m, gm[m, k], row)
            value = jnp.where(a_in == k, row[:1], value)
        value = value * sign * (1.0 / 64.0)
        hi = value.astype(BF)
        rows = pl.ds(pl.multiple_of(i * 128, 128), 128)
        mhi[rows, :] = hi
        mlo[rows, :] = (value - hi.astype(F32)).astype(BF)
        return carry

    lax.fori_loop(0, TILES, build, 0)

    act_first_done(0)
    act_a(0)
    act_first_done(1)
    act_a(1)
    act_b(0)
    act_first_done(2)
    act_a(2)
    act_b(1)
    act_sib(0)
    act_first_done(3)
    act_a(3)
    act_b(2)
    down_start()
    wait_for(wv, w_sem)
    act_done(0)
    multiply(0)
    act_sib(1)
    act_b(3)
    act_done(1)
    multiply(1)
    act_sib(2)
    relay(0)
    act_done(2)
    multiply(2)
    act_sib(3)
    relay(1)
    hide(0)
    act_done(3)
    multiply(3)
    relay(2)
    hide(1)
    relay(3)
    hide_sib(0)
    mix(0)
    hide(2)
    hide(3)
    wait_for(dv, d_sem)
    project(0)
    hide_sib(1)
    mix(1)
    gather_one(0)
    project(1)
    finish(0)
    gather_one(1)
    finish(1)
    for r in range(CHUNKS):
        act_sent(r)
        reduce_sent(r)
    for r in range(PARTS):
        mix_sent(r)
        project_sent(r)


def local(activations, gate_weight, up_weight, group_mix, down_weight):
    any_space = pl.BlockSpec(memory_space=pl.ANY)
    dma = pltpu.SemaphoreType.DMA
    vm = pltpu.VMEM
    r, n = CHUNKS, PARTS
    scratch = [
        vm((TILES, 2, 4, 256, 256), BF),
        vm((16, SPAN, 512), BF),
        vm((r, 4, 4, Q, 2048), BF),
        vm((4, RB, 256), F32),
        vm((r, TILES, RB, 256), F32),
        vm((r, 2, TILES, HB, 256), F32),
        vm((r, TILES, 2, HB, 256), BF),
        vm((r, 2, TILES, 2, HB, 256), BF),
        vm((r, 2, TILES, HB, 256), BF),
        vm((r, 2, TILES, 2, HB, 256), BF),
        vm((SPAN, SPAN), BF),
        vm((SPAN, SPAN), BF),
        vm((n, 16, 64, 128), BF),
        vm((n, 2, 16, 64, 128), BF),
        vm((n, 16, 64, 128), BF),
        vm((n, 16, 64, 128), BF),
        vm((RT, SPAN), BF),
        vm((n, 16, RT, 256), BF),
        vm((16, RT, 256), F32),
        vm((n, 16, RT, 256), BF),
        vm((n, 2, 4, 4, HT, 256), BF),
        vm((n, 2, 3, 4, HT, 256), BF),
        vm((n, 2, 4, HT, 256), BF),
        vm((n, 2, 3, HT, 256), BF),
        dma(()), dma(()),
        dma((r, 4)), dma((r,)),
        dma((r, 5)), dma((r, 5)),
        dma((r,)), dma((r, 2, TILES)),
        dma((r,)), dma((r, 2)),
        dma((n, 3)), dma((n, 3)),
        dma((n,)), dma((n, 16)),
        dma((n, 4)), dma((n, 4)),
    ]
    return pl.pallas_call(
        kernel,
        out_shape=jax.ShapeDtypeStruct((256, 256), BF),
        in_specs=[any_space, any_space, any_space, pl.BlockSpec(memory_space=pltpu.SMEM), any_space],
        out_specs=pl.BlockSpec(memory_space=pltpu.VMEM),
        scratch_shapes=scratch,
        compiler_params=pltpu.CompilerParams(
            collective_id=0, has_side_effects=True, vmem_limit_bytes=60 * 1024 * 1024
        ),
        cost_estimate=pl.CostEstimate(flops=12_000_000_000, bytes_accessed=24_000_000, transcendentals=230_000),
        name="ffn",
    )(
        activations,
        gate_weight.reshape(4, 2, 256, SPAN),
        up_weight.reshape(4, 2, 256, SPAN),
        group_mix,
        down_weight,
    )


def solution(mesh):
    return jax.shard_map(
        local,
        mesh=mesh,
        in_specs=(P("dp", "tensor"), P("dp", "tensor"), P("dp", "tensor"), P(), P("tensor", None)),
        out_specs=P("dp", "tensor"),
        check_vma=False,
    )
```

```python
import jax
import jax.numpy as jnp
from jax import lax
from jax.experimental import pallas as pl
from jax.experimental.pallas import tpu as pltpu
from jax.sharding import PartitionSpec as P

MESH = pl.DeviceIdType.MESH
BF = jnp.bfloat16
F32 = jnp.float32

CHUNKS = 4
RB = 256 // CHUNKS
PARTS = ((0, 1), (2,), (3,))
PART_OF = [k for k, part in enumerate(PARTS) for _ in part]
ROWS = [RB * len(part) for part in PARTS]
OFF = [RB * part[0] for part in PARTS]
LAST = len(PARTS) - 1
PIECE = [rows // 16 for rows in ROWS]
PK = [8 * piece for piece in PIECE]
Q = RB // 4
HB = RB // 2
TILES = 7
SPAN = 896
LAG = 4
GROUPS = 8


def wait_for(ref, sem):
    pltpu.make_async_copy(ref, ref, sem).wait()


def cross(a, b):
    low = lax.broadcasted_iota(jnp.int32, a.shape, a.ndim - 2) < 4
    half_turn = lambda v: jnp.concatenate([v[..., 4:, :], v[..., :4, :]], axis=-2)
    return jnp.where(low, a, half_turn(b)), jnp.where(low, half_turn(a), b)


def pack(groups, piece):
    rows = groups[0].shape[0]
    groups = [g.reshape(rows // 8, 8, 128) for g in groups]
    groups.append(jnp.zeros_like(groups[0]))
    if piece == 8:
        pairs = [jnp.concatenate(groups[i : i + 2], axis=1) for i in range(0, GROUPS, 2)]
        return jnp.concatenate([v.astype(BF) for v in pairs], axis=1)
    even, odd = zip(*[cross(groups[i], groups[i + 1]) for i in range(0, GROUPS, 2)])
    both = jnp.stack([jnp.concatenate(even, axis=1), jnp.concatenate(odd, axis=1)], axis=1)
    return both.reshape(rows // 4, 32, 128).astype(BF)


def unpack(packed, piece):
    out = []
    if piece == 8:
        for i in range(0, GROUPS, 2):
            pair = packed[:, i * 8 : i * 8 + 16, :].astype(F32)
            out += [pair[:, :8, :].reshape(128, 128), pair[:, 8:, :].reshape(128, 128)]
    else:
        both = packed.astype(F32).reshape(8, 2, 32, 128)
        for i in range(0, GROUPS, 2):
            rows = slice(4 * i, 4 * i + 8)
            first, second = cross(both[:, 0, rows], both[:, 1, rows])
            out += [first.reshape(64, 128), second.reshape(64, 128)]
    return jnp.concatenate([v.astype(BF) for v in out[:TILES]], axis=1)


def kernel(
    act, gate, up, gm, down, out,
    wv, dv, af, pacc, own, nb, xo, xn, ro, rn,
    mhi, mlo, hs, hr, rs, rr, rot, ds, dk, dr, es, f1, g2, f2, ed, fd,
    w_sem, d_sem, a1_s, a1_r, ag_s, ag_r, xo_s, xo_r, xn_s, xn_r,
    h_s, h_r, ds_s, ds_r, e_s, e_r, a0_r, ao_s, ao_r,
):
    x = lax.axis_index("dp")
    t = lax.axis_index("tensor")
    y, z, c = t // 8, (t // 2) % 4, t % 2
    p = t // 2
    sib = 1 - c
    xp, xm = (x + 1) % 4, (x + 3) % 4
    kb, kbs = c * 4 + z, pl.ds(c * 4, 4)

    def at(x_, y_, z_, c_):
        return (x_, y_ * 8 + z_ * 2 + c_)

    def send(src, dst, ss, rs_, dev):
        pltpu.make_async_remote_copy(
            src_ref=src, dst_ref=dst, send_sem=ss, recv_sem=rs_, device_id=dev, device_id_type=MESH
        ).start()

    for j in range(TILES):
        for cc in range(2):
            cols = pl.ds(j * 128, 128)
            pltpu.make_async_copy(gate.at[:, cc, :, cols], wv.at[j, cc, :, :, pl.ds(0, 128)], w_sem).start()
            pltpu.make_async_copy(up.at[:, cc, :, cols], wv.at[j, cc, :, :, pl.ds(128, 128)], w_sem).start()
    bar = pltpu.get_barrier_semaphore()

    def greet(dev):
        pl.semaphore_signal(bar, inc=1, device_id=dev, device_id_type=MESH)

    same = x == y
    greet((xp, t))
    greet((xm, t))
    greet(at(x, y, z, sib))
    for k in range(4):
        @pl.when(jnp.logical_not(jnp.logical_and(same, y == k)))
        def _():
            greet(at(y, k, z, c))

        @pl.when(jnp.logical_not(jnp.logical_and(same, x == k)))
        def _():
            greet(at(k, x, z, c))


    def greet_plane(i, carry):
        greet((x, (p + i) % 16 * 2 + c))
        return carry

    lax.fori_loop(1, 16, greet_plane, 0)
    pl.semaphore_wait(bar, jnp.where(same, 24, 26))

    def down_start():
        for j in range(16):
            pltpu.make_async_copy(down.at[:, pl.ds(j * 512, 512)], dv.at[j], d_sem).start()

    def act_first(r):
        sem = a0_r.at[x] if r == 0 else a1_r.at[r]
        for k in range(4):
            src = act.at[pl.ds(r * RB + k * Q, Q), :]
            dst = af.at[r, x, kb, k]
            here = jnp.logical_and(same, y == k)

            @pl.when(here)
            def _():
                pltpu.make_async_copy(src, dst, sem).start()

            @pl.when(jnp.logical_not(here))
            def _():
                send(src, dst, a1_s.at[r, k], sem, at(y, k, z, c))

    def act_first_done(r):
        wait_for(af.at[r, :, 0, 0], a1_r.at[r])

    def act_a(r):
        for i in range(1, 4):
            piece = af.at[r, pl.ds(0, 2), kb, y]
            send(piece, piece, ag_s.at[r, 0], ag_r.at[r, 0], at(x, (y + i) % 4, z, c))
            piece = af.at[r, pl.ds(2, 2), kb, y]
            send(piece, piece, ag_s.at[r, 1], ag_r.at[r, 1], at(x, y, (z + i) % 4, c))

    def act_b(r):
        wait_for(af.at[r, pl.ds(0, 2), 0, pl.ds(0, 3)], ag_r.at[r, 0])
        for i in range(1, 4):
            piece = af.at[r, pl.ds(0, 2), kb]
            send(piece, piece, ag_s.at[r, 2], ag_r.at[r, 2], at(x, y, (z + i) % 4, c))
        wait_for(af.at[r, pl.ds(0, 2), 0, pl.ds(0, 3)], ag_r.at[r, 1])
        for i in range(1, 4):
            piece = af.at[r, pl.ds(2, 2), kbs, y]
            send(piece, piece, ag_s.at[r, 3], ag_r.at[r, 3], at(x, (y + i) % 4, z, c))

    def act_sib(r):
        wait_for(af.at[r, pl.ds(0, 2), pl.ds(0, 3)], ag_r.at[r, 2])
        wait_for(af.at[r, pl.ds(0, 2), pl.ds(0, 3)], ag_r.at[r, 3])
        piece = af.at[r, :, kbs]
        send(piece, piece, ag_s.at[r, 4], ag_r.at[r, 4], at(x, y, z, sib))

    def block(i):
        a, b = i // 4, i % 4
        dy, dz = (3 * a * a + 3 * a + 6) % 7 % 4, (3 * b * b + 3 * b + 6) % 7 % 4
        return ((y + dy) % 4) * 4 + (z + dz) % 4

    def own0_first(o):
        wait_for(af.at[0, 0, 0, 0], a0_r.at[(x + o) % 4])

    def own0_a(o):
        piece = af.at[0, (x + o) % 4, kb, y]

        def step(i, carry):
            send(piece, piece, ao_s.at[o, 0], ao_r.at[o, 0], (x, block(i) * 2 + c))
            return carry

        lax.fori_loop(0, 15, step, 0)

    def own0_sib(o):
        wait_for(af.at[0, pl.ds(0, 3), pl.ds(0, 5), 0], ao_r.at[o, 0])
        piece = af.at[0, (x + o) % 4, kbs]
        send(piece, piece, ao_s.at[o, 1], ao_r.at[o, 1], at(x, y, z, sib))

    def own0_done(o):
        wait_for(af.at[0, 0, pl.ds(0, 4)], ao_r.at[o, 1])

    def act_done(r):
        wait_for(af.at[r, :, pl.ds(0, 4)], ag_r.at[r, 4])

    def act_sent(r):
        for k in range(4):
            @pl.when(jnp.logical_not(jnp.logical_and(same, y == k)))
            def _():
                wait_for(af.at[r, 0, 0, 0], a1_s.at[r, k])
        if r == 0:
            for o in range(4):
                wait_for(af.at[0, pl.ds(0, 3), pl.ds(0, 5), 0], ao_s.at[o, 0])
                wait_for(af.at[0, 0, pl.ds(0, 4)], ao_s.at[o, 1])
            return
        wait_for(af.at[r, pl.ds(0, 2), 0, pl.ds(0, 3)], ag_s.at[r, 0])
        wait_for(af.at[r, pl.ds(0, 2), 0, pl.ds(0, 3)], ag_s.at[r, 1])
        wait_for(af.at[r, pl.ds(0, 2), pl.ds(0, 3)], ag_s.at[r, 2])
        wait_for(af.at[r, pl.ds(0, 2), pl.ds(0, 3)], ag_s.at[r, 3])
        wait_for(af.at[r, :, pl.ds(0, 4)], ag_s.at[r, 4])

    def direct_tile(r, j):
        send(xn.at[r, 0, j, 1], rn.at[r, 0, j, 1], xn_s.at[r], xn_r.at[r, 0], (xp, t))
        send(xn.at[r, 1, j, 0], rn.at[r, 1, j, 0], xn_s.at[r], xn_r.at[r, 1], (xm, t))

    def far_tile(r, j, far):
        xo[r, j, 0] = far[:HB]
        xo[r, j, 1] = far[HB:]
        send(xo.at[r, j, 0], ro.at[r, 0, j], xo_s.at[r], xo_r.at[r, 0, j], (xp, t))
        send(xo.at[r, j, 1], ro.at[r, 1, j], xo_s.at[r], xo_r.at[r, 1, j], (xm, t))

    def multiply_far(r, start, stop):
        def step(j, carry):
            a = jnp.concatenate([af[r, (x + 2) % 4, b].reshape(RB, 256) for b in range(8)], axis=1)
            far_tile(r, j, jnp.dot(a, wv[j].reshape(2048, 256), preferred_element_type=F32).astype(BF))
            return carry

        lax.fori_loop(start, stop, step, 0)

    def multiply(r, at_once):
        def step(j, carry):
            w = wv[j].reshape(2048, 256)
            a = jnp.concatenate([af[r, :, b].reshape(4 * RB, 256) for b in range(8)], axis=1)
            pacc[...] = jnp.dot(a, w, preferred_element_type=F32).reshape(4, RB, 256)
            if r > 0:
                far_tile(r, j, pacc[(x + 2) % 4].astype(BF))
            nxt = pacc[xp]
            nb[r, 0, j] = nxt[:HB]
            xn[r, 0, j, 1] = nxt[HB:].astype(BF)
            prv = pacc[xm]
            nb[r, 1, j] = prv[HB:]
            xn[r, 1, j, 0] = prv[:HB].astype(BF)
            if at_once:
                direct_tile(r, j)
            own[r, j] = pacc[x]
            return carry

        lax.fori_loop(0, TILES, step, 0)

    def direct(r):
        def step(j, carry):
            direct_tile(r, j)
            return carry

        lax.fori_loop(0, TILES, step, 0)

    def relay(r):
        def step(j, carry):
            wait_for(ro.at[r, 0, j], xo_r.at[r, 0, j])
            xn[r, 0, j, 0] = (nb[r, 0, j] + ro[r, 0, j].astype(F32)).astype(BF)
            send(xn.at[r, 0, j, 0], rn.at[r, 0, j, 0], xn_s.at[r], xn_r.at[r, 0], (xp, t))
            wait_for(ro.at[r, 1, j], xo_r.at[r, 1, j])
            xn[r, 1, j, 1] = (nb[r, 1, j] + ro[r, 1, j].astype(F32)).astype(BF)
            send(xn.at[r, 1, j, 1], rn.at[r, 1, j, 1], xn_s.at[r], xn_r.at[r, 1], (xm, t))
            return carry

        lax.fori_loop(0, TILES, step, 0)

    def reduce_sent(r):
        wait_for(xo.at[r], xo_s.at[r])
        wait_for(xn.at[r], xn_s.at[r])

    def pieces(ref, k, count):
        return ref.at[k, pl.ds(0, count * PK[k])]

    def piece_of(k, q):
        return pl.ds(pl.multiple_of(q * PK[k], PK[k]), PK[k])

    def hide(r):
        k = PART_OF[r]
        count = RB // PIECE[k]
        first = (r - PARTS[k][0]) * count
        wait_for(rn.at[r, 0], xn_r.at[r, 0])
        wait_for(rn.at[r, 1], xn_r.at[r, 1])
        groups = []
        for j in range(TILES):
            s = own[r, j] + rn[r, 0, j].reshape(RB, 256).astype(F32) + rn[r, 1, j].reshape(RB, 256).astype(F32)
            g, u = s[:, :128], s[:, 128:]
            groups.append(g / (1.0 + jnp.exp(-g)) * u)
        hs[k, pl.ds(first * PK[k], count * PK[k])] = pack(groups, PIECE[k]).reshape(count * PK[k], 128)
        mine = piece_of(k, p)

        def step(i, carry):
            q = first + (p + i) % count

            @pl.when(q != p)
            def _():
                send(hs.at[k, piece_of(k, q)], hr.at[k, c, mine], h_s.at[k, 0], h_r.at[k, 0], (x, q * 2 + c))

            @pl.when(q == p)
            def _():
                hr[k, c, mine] = hs[k, mine]

            return carry

        lax.fori_loop(0, count, step, 0)

    def hide_sib(k):
        wait_for(pieces(hs, k, 15), h_r.at[k, 0])
        both = hr.at[k, c, pl.ds(0, 16 * PK[k])]
        send(both, both, h_s.at[k, 1], h_r.at[k, 1], at(x, y, z, sib))

    def mix(k):
        n, piece, every, mine = ROWS[k], PIECE[k], pl.ds(0, 16 * PK[k]), piece_of(k, p)
        wait_for(pieces(hs, k, 16), h_r.at[k, 1])
        both = jnp.concatenate([unpack(hr[k, i, every].reshape(16, PK[k], 128), piece) for i in range(2)], axis=0)
        mixed = jnp.dot(both, mhi[...], preferred_element_type=F32)
        mixed = mixed + jnp.dot(both, mlo[...], preferred_element_type=F32)
        sign = jnp.where(c == 0, 1.0, -1.0).astype(F32)
        s = mixed[:n] + sign * mixed[n:]
        if piece == 4:
            v = s.reshape(8, 8, SPAN)
            turned = jnp.concatenate([v[:, 4:], v[:, :4]], axis=1)
            low = lax.broadcasted_iota(jnp.int32, v.shape, 1) < 4
            s = jnp.where(low, v + turned, turned - v).reshape(n, SPAN)
        parts = [s[8 * i : 8 * i + 8] for i in range(n // 8)]
        half = 1
        while half < len(parts):
            for i in range(len(parts)):
                if i & half == 0:
                    a, b = parts[i], parts[i + half]
                    parts[i], parts[i + half] = a + b, a - b
            half *= 2
        for i in range(len(parts)):
            groups = [parts[i][:, 128 * g : 128 * g + 128] for g in range(TILES)]
            rs[k, pl.ds(i * 64, 64)] = pack(groups, piece).reshape(64, 128)
        rr[k, mine] = rs[k, mine]

        def step(i, carry):
            q = (p + i) % 16
            send(rs.at[k, piece_of(k, q)], rr.at[k, mine], h_s.at[k, 2], h_r.at[k, 2], (x, q * 2 + c))
            return carry

        lax.fori_loop(1, 16, step, 0)

    def mix_sent(k):
        wait_for(pieces(hs, k, 15), h_s.at[k, 0])
        wait_for(pieces(hs, k, 16), h_s.at[k, 1])
        wait_for(pieces(hs, k, 15), h_s.at[k, 2])

    def spread(k, i):
        h, rows, halves, top = ROWS[k] // 2, pl.ds(OFF[k], ROWS[k]), pl.ds(OFF[k] // 2, ROWS[k] // 2), pl.ds(0, ROWS[k])
        q = block(i)
        qy, qz = q // 4, q % 4
        wait_for(dr.at[q, rows], ds_r.at[k, q])
        e = (dk[q, top] + dr[q, rows].astype(F32)).astype(BF)
        if k == LAST:
            ed[q] = e

            @pl.when(i < 15)
            def _():
                send(ed.at[q], fd.at[p], e_s.at[k, 0], e_r.at[k, 0], (x, q * 2 + c))

            return
        es[0, qy, qz, halves] = e[:h]
        es[1, qy, qz, halves] = e[h:]

        @pl.when(qz != z)
        def _():
            slot = (qz + 3 - z) % 4
            dst = f1.at[0, slot, qy, halves]
            send(es.at[0, qy, qz, halves], dst, e_s.at[k, 0], e_r.at[k, 0], at(x, y, qz, c))

        @pl.when(qy != y)
        def _():
            slot = (qy + 3 - y) % 4
            dst = f1.at[1, slot, qz, halves]
            send(es.at[1, qy, qz, halves], dst, e_s.at[k, 1], e_r.at[k, 1], at(x, qy, z, c))

    def project(k, start, stop):
        rows, top = pl.ds(OFF[k], ROWS[k]), pl.ds(0, ROWS[k])
        if start == 0:
            wait_for(pieces(rr, k, 15), h_r.at[k, 2])
            rot[top, :] = unpack(rr[k, pl.ds(0, 16 * PK[k])].reshape(16, PK[k], 128), PIECE[k])

        def step(i, carry):
            q = block(i)
            d = jnp.dot(rot[top, :], dv[q], preferred_element_type=F32)
            left, right = d[:, :256], d[:, 256:]
            dk[q, top] = jnp.where(c == 0, left, right)
            ds[q, rows] = jnp.where(c == 0, right, left).astype(BF)
            send(ds.at[q, rows], dr.at[q, rows], ds_s.at[k], ds_r.at[k, q], at(x, y, z, sib))

            @pl.when(i >= LAG)
            def _():
                spread(k, i - LAG)

            return carry

        lax.fori_loop(start, stop, step, 0)

    def flush(k):
        def step(i, carry):
            spread(k, i)
            return carry

        lax.fori_loop(16 - LAG, 16, step, 0)

    def gather_one(k):
        halves = pl.ds(OFF[k] // 2, ROWS[k] // 2)
        for a in range(2):
            wait_for(f1.at[a, :, :, halves], e_r.at[k, a])
            total = es[0, :, z, halves].astype(F32) if a == 0 else es[1, y, :, halves].astype(F32)
            for i in range(3):
                total = total + f1[a, i, :, halves].astype(F32)
            g2[a, :, halves] = total.astype(BF)
            for i in range(1, 4):
                q = (y + i) % 4 if a == 0 else (z + i) % 4
                dev = at(x, q, z, c) if a == 0 else at(x, y, q, c)
                send(g2.at[a, q, halves], f2.at[a, i - 1, halves], e_s.at[k, 2 + a], e_r.at[k, 2 + a], dev)

    def finish(k):
        h = ROWS[k] // 2
        if k == LAST:
            wait_for(ed.at[pl.ds(0, 15)], e_r.at[k, 0])
            fd[p] = ed[p]
            total = fd[0].astype(F32)
            for i in range(1, 16):
                total = total + fd[i].astype(F32)
            out[pl.ds(OFF[k], ROWS[k]), :] = total.astype(BF)
            return
        halves = pl.ds(OFF[k] // 2, h)
        for a, own_block in ((0, y), (1, z)):
            wait_for(f2.at[a, :, halves], e_r.at[k, 2 + a])
            total = g2[a, own_block, halves].astype(F32)
            for i in range(3):
                total = total + f2[a, i, halves].astype(F32)
            out[pl.ds(OFF[k] + a * h, h), :] = total.astype(BF)

    def project_sent(k):
        halves = pl.ds(OFF[k] // 2, ROWS[k] // 2)
        wait_for(ds.at[:, pl.ds(OFF[k], ROWS[k])], ds_s.at[k])
        if k == LAST:
            wait_for(ed.at[pl.ds(0, 15)], e_s.at[k, 0])
            return
        for a in range(2):
            wait_for(f1.at[a, :, :, halves], e_s.at[k, a])
            wait_for(f2.at[a, :, halves], e_s.at[k, 2 + a])

    for r in range(CHUNKS):
        act_first(r)

    def build(i, carry):
        f_in = i * 128 + lax.broadcasted_iota(jnp.int32, (128, SPAN), 0)
        f_out = lax.broadcasted_iota(jnp.int32, (128, SPAN), 1)
        b_in, b_out = (f_in * 9363) >> 16, (f_out * 9363) >> 16
        a_in, a_out = f_in - 7 * b_in, f_out - 7 * b_out
        v = b_in & b_out
        v = v ^ (v >> 4)
        v = v ^ (v >> 2)
        v = v ^ (v >> 1)
        sign = (1 - 2 * (v & 1)).astype(F32)
        value = jnp.zeros((128, SPAN), F32)
        a_row = a_out[:8]
        for k in range(7):
            row = jnp.zeros((8, SPAN), F32)
            for m in range(7):
                row = jnp.where(a_row == m, gm[m, k], row)
            value = jnp.where(a_in == k, row[:1], value)
        value = value * sign * (1.0 / 64.0)
        hi = value.astype(BF)
        rows = pl.ds(pl.multiple_of(i * 128, 128), 128)
        mhi[rows, :] = hi
        mlo[rows, :] = (value - hi.astype(F32)).astype(BF)
        return carry

    lax.fori_loop(0, TILES, build, 0)

    own0_first(2)
    own0_a(2)
    own0_first(1)
    own0_a(1)
    own0_first(3)
    own0_a(3)
    own0_first(0)
    own0_a(0)
    act_first_done(1)
    act_a(1)
    act_first_done(2)
    act_a(2)
    act_first_done(3)
    act_a(3)
    wait_for(wv, w_sem)
    own0_sib(2)
    own0_sib(1)
    own0_sib(3)
    act_b(1)
    own0_done(2)
    multiply_far(0, 0, 3)
    own0_sib(0)
    act_b(2)
    multiply_far(0, 3, 7)
    act_b(3)
    own0_done(1)
    own0_done(3)
    own0_done(0)
    multiply(0, True)
    act_sib(1)
    relay(0)
    act_sib(2)
    act_done(1)
    multiply(1, True)
    act_sib(3)
    act_done(2)
    multiply(2, False)
    relay(1)
    direct(2)
    hide(0)
    act_done(3)
    multiply(3, False)
    down_start()
    relay(2)
    direct(3)
    hide(1)
    relay(3)
    hide_sib(0)
    mix(0)
    hide(2)
    hide(3)
    hide_sib(1)
    mix(1)
    wait_for(dv, d_sem)
    project(0, 0, 8)
    hide_sib(2)
    project(0, 8, 12)
    mix(2)
    project(0, 12, 16)
    project(1, 0, 4)
    flush(0)
    project(1, 4, 16)
    gather_one(0)
    project(2, 0, 4)
    flush(1)
    project(2, 4, 16)
    flush(2)
    finish(0)
    gather_one(1)
    finish(1)
    finish(2)
    for r in range(CHUNKS):
        act_sent(r)
        reduce_sent(r)
    for r in range(len(PARTS)):
        mix_sent(r)
        project_sent(r)


def local(activations, gate_weight, up_weight, group_mix, down_weight):
    any_space = pl.BlockSpec(memory_space=pl.ANY)
    dma = pltpu.SemaphoreType.DMA
    vm = pltpu.VMEM
    r, n = CHUNKS, len(PARTS)
    scratch = [
        vm((TILES, 2, 4, 256, 256), BF),
        vm((16, SPAN, 512), BF),
        vm((r, 4, 8, 4, Q, 256), BF),
        vm((4, RB, 256), F32),
        vm((r, TILES, RB, 256), F32),
        vm((r, 2, TILES, HB, 256), F32),
        vm((r, TILES, 2, HB, 256), BF),
        vm((r, 2, TILES, 2, HB, 256), BF),
        vm((r, 2, TILES, HB, 256), BF),
        vm((r, 2, TILES, 2, HB, 256), BF),
        vm((SPAN, SPAN), BF),
        vm((SPAN, SPAN), BF),
        vm((n, 16 * 64, 128), BF),
        vm((n, 2, 16 * 64, 128), BF),
        vm((n, 16 * 64, 128), BF),
        vm((n, 16 * 64, 128), BF),
        vm((128, SPAN), BF),
        vm((16, 256, 256), BF),
        vm((16, 128, 256), F32),
        vm((16, 256, 256), BF),
        vm((2, 4, 4, 128, 256), BF),
        vm((2, 3, 4, 128, 256), BF),
        vm((2, 4, 128, 256), BF),
        vm((2, 3, 128, 256), BF),
        vm((16, ROWS[-1], 256), BF),
        vm((16, ROWS[-1], 256), BF),
        dma(()), dma(()),
        dma((r, 4)), dma((r,)),
        dma((r, 5)), dma((r, 5)),
        dma((r,)), dma((r, 2, TILES)),
        dma((r,)), dma((r, 2)),
        dma((n, 3)), dma((n, 3)),
        dma((n,)), dma((n, 16)),
        dma((n, 4)), dma((n, 4)),
        dma((4,)), dma((4, 2)), dma((4, 2)),
    ]
    return pl.pallas_call(
        kernel,
        out_shape=jax.ShapeDtypeStruct((256, 256), BF),
        in_specs=[any_space, any_space, any_space, pl.BlockSpec(memory_space=pltpu.SMEM), any_space],
        out_specs=pl.BlockSpec(memory_space=pltpu.VMEM),
        scratch_shapes=scratch,
        compiler_params=pltpu.CompilerParams(
            collective_id=0, has_side_effects=True, vmem_limit_bytes=60 * 1024 * 1024
        ),
        cost_estimate=pl.CostEstimate(flops=12_000_000_000, bytes_accessed=24_000_000, transcendentals=230_000),
        name="ffn",
    )(
        activations,
        gate_weight.reshape(4, 2, 256, SPAN),
        up_weight.reshape(4, 2, 256, SPAN),
        group_mix,
        down_weight,
    )


def solution(mesh):
    return jax.shard_map(
        local,
        mesh=mesh,
        in_specs=(P("dp", "tensor"), P("dp", "tensor"), P("dp", "tensor"), P(), P("tensor", None)),
        out_specs=P("dp", "tensor"),
        check_vma=False,
    )
```

```python
import jax
import jax.numpy as jnp
from jax import lax
from jax.experimental import pallas as pl
from jax.experimental.pallas import tpu as pltpu
from jax.sharding import PartitionSpec as P

MESH = pl.DeviceIdType.MESH
BF = jnp.bfloat16
F32 = jnp.float32

CHUNKS = 4
RB = 256 // CHUNKS
PARTS = ((0, 1), (2,), (3,))
PART_OF = [k for k, part in enumerate(PARTS) for _ in part]
ROWS = [RB * len(part) for part in PARTS]
OFF = [RB * part[0] for part in PARTS]
LAST = len(PARTS) - 1
PIECE = [rows // 16 for rows in ROWS]
PK = [8 * piece for piece in PIECE]
Q = RB // 4
HB = RB // 2
TILES = 7
SPAN = 896
LAG = 3
GROUPS = 8


def wait_for(ref, sem):
    pltpu.make_async_copy(ref, ref, sem).wait()


def cross(a, b):
    low = lax.broadcasted_iota(jnp.int32, a.shape, a.ndim - 2) < 4
    half_turn = lambda v: jnp.concatenate([v[..., 4:, :], v[..., :4, :]], axis=-2)
    return jnp.where(low, a, half_turn(b)), jnp.where(low, half_turn(a), b)


def pack(groups, piece):
    rows = groups[0].shape[0]
    groups = [g.reshape(rows // 8, 8, 128) for g in groups]
    groups.append(jnp.zeros_like(groups[0]))
    if piece == 8:
        pairs = [jnp.concatenate(groups[i : i + 2], axis=1) for i in range(0, GROUPS, 2)]
        return jnp.concatenate([v.astype(BF) for v in pairs], axis=1)
    even, odd = zip(*[cross(groups[i], groups[i + 1]) for i in range(0, GROUPS, 2)])
    both = jnp.stack([jnp.concatenate(even, axis=1), jnp.concatenate(odd, axis=1)], axis=1)
    return both.reshape(rows // 4, 32, 128).astype(BF)


def unpack(packed, piece):
    out = []
    if piece == 8:
        for i in range(0, GROUPS, 2):
            pair = packed[:, i * 8 : i * 8 + 16, :].astype(F32)
            out += [pair[:, :8, :].reshape(128, 128), pair[:, 8:, :].reshape(128, 128)]
    else:
        both = packed.astype(F32).reshape(8, 2, 32, 128)
        for i in range(0, GROUPS, 2):
            rows = slice(4 * i, 4 * i + 8)
            first, second = cross(both[:, 0, rows], both[:, 1, rows])
            out += [first.reshape(64, 128), second.reshape(64, 128)]
    return jnp.concatenate([v.astype(BF) for v in out[:TILES]], axis=1)


def kernel(
    act, gate, up, gm, down, out,
    wv, dv, af, pacc, own, nb, xo, xn, ro, rn,
    mhi, mlo, hs, hr, rs, rr, rot, ds, dk, dr, es, f1, g2, f2, ed, fd,
    w_sem, d_sem, a1_s, a1_r, ag_s, ag_r, xo_s, xo_r, xn_s, xn_r,
    h_s, h_r, ds_s, ds_r, e_s, e_r, a0_r, ao_s, ao_r,
):
    x = lax.axis_index("dp")
    t = lax.axis_index("tensor")
    y, z, c = t // 8, (t // 2) % 4, t % 2
    p = t // 2
    sib = 1 - c
    xp, xm = (x + 1) % 4, (x + 3) % 4
    kb, kbs = c * 4 + z, pl.ds(c * 4, 4)

    def at(x_, y_, z_, c_):
        return (x_, y_ * 8 + z_ * 2 + c_)

    def send(src, dst, ss, rs_, dev):
        pltpu.make_async_remote_copy(
            src_ref=src, dst_ref=dst, send_sem=ss, recv_sem=rs_, device_id=dev, device_id_type=MESH
        ).start()

    for j in range(TILES):
        for cc in range(2):
            cols = pl.ds(j * 128, 128)
            pltpu.make_async_copy(gate.at[:, cc, :, cols], wv.at[j, cc, :, :, pl.ds(0, 128)], w_sem).start()
            pltpu.make_async_copy(up.at[:, cc, :, cols], wv.at[j, cc, :, :, pl.ds(128, 128)], w_sem).start()
    bar = pltpu.get_barrier_semaphore()

    def greet(dev):
        pl.semaphore_signal(bar, inc=1, device_id=dev, device_id_type=MESH)

    same = x == y
    greet((xp, t))
    greet((xm, t))
    greet(at(x, y, z, sib))
    for k in range(4):
        @pl.when(jnp.logical_not(jnp.logical_and(same, y == k)))
        def _():
            greet(at(y, k, z, c))

        @pl.when(jnp.logical_not(jnp.logical_and(same, x == k)))
        def _():
            greet(at(k, x, z, c))


    def greet_plane(i, carry):
        greet((x, (p + i) % 16 * 2 + c))
        return carry

    lax.fori_loop(1, 16, greet_plane, 0)
    pl.semaphore_wait(bar, jnp.where(same, 24, 26))

    def down_start():
        for j in range(16):
            pltpu.make_async_copy(down.at[:, pl.ds(j * 512, 512)], dv.at[j], d_sem).start()

    def act_first(r):
        sem = a0_r.at[x] if r == 0 else a1_r.at[r]
        for k in range(4):
            src = act.at[pl.ds(r * RB + k * Q, Q), :]
            dst = af.at[r, x, kb, k]
            here = jnp.logical_and(same, y == k)

            @pl.when(here)
            def _():
                pltpu.make_async_copy(src, dst, sem).start()

            @pl.when(jnp.logical_not(here))
            def _():
                send(src, dst, a1_s.at[r, k], sem, at(y, k, z, c))

    def act_first_done(r):
        wait_for(af.at[r, :, 0, 0], a1_r.at[r])

    def act_a(r):
        for i in range(1, 4):
            piece = af.at[r, pl.ds(0, 2), kb, y]
            send(piece, piece, ag_s.at[r, 0], ag_r.at[r, 0], at(x, (y + i) % 4, z, c))
            piece = af.at[r, pl.ds(2, 2), kb, y]
            send(piece, piece, ag_s.at[r, 1], ag_r.at[r, 1], at(x, y, (z + i) % 4, c))

    def act_b(r):
        wait_for(af.at[r, pl.ds(0, 2), 0, pl.ds(0, 3)], ag_r.at[r, 0])
        for i in range(1, 4):
            piece = af.at[r, pl.ds(0, 2), kb]
            send(piece, piece, ag_s.at[r, 2], ag_r.at[r, 2], at(x, y, (z + i) % 4, c))
        wait_for(af.at[r, pl.ds(0, 2), 0, pl.ds(0, 3)], ag_r.at[r, 1])
        for i in range(1, 4):
            piece = af.at[r, pl.ds(2, 2), kbs, y]
            send(piece, piece, ag_s.at[r, 3], ag_r.at[r, 3], at(x, (y + i) % 4, z, c))

    def act_sib(r):
        wait_for(af.at[r, pl.ds(0, 2), pl.ds(0, 3)], ag_r.at[r, 2])
        wait_for(af.at[r, pl.ds(0, 2), pl.ds(0, 3)], ag_r.at[r, 3])
        piece = af.at[r, :, kbs]
        send(piece, piece, ag_s.at[r, 4], ag_r.at[r, 4], at(x, y, z, sib))

    def block(i):
        a, b = i // 4, i % 4
        dy, dz = (3 * a * a + 3 * a + 6) % 7 % 4, (3 * b * b + 3 * b + 6) % 7 % 4
        return ((y + dy) % 4) * 4 + (z + dz) % 4

    def own0_first(o):
        wait_for(af.at[0, 0, 0, 0], a0_r.at[(x + o) % 4])

    def own0_a(o):
        piece = af.at[0, (x + o) % 4, kb, y]

        def step(i, carry):
            send(piece, piece, ao_s.at[o, 0], ao_r.at[o, 0], (x, block(i) * 2 + c))
            return carry

        lax.fori_loop(0, 15, step, 0)

    def own0_sib(o):
        wait_for(af.at[0, pl.ds(0, 3), pl.ds(0, 5), 0], ao_r.at[o, 0])
        piece = af.at[0, (x + o) % 4, kbs]
        send(piece, piece, ao_s.at[o, 1], ao_r.at[o, 1], at(x, y, z, sib))

    def own0_done(o):
        wait_for(af.at[0, 0, pl.ds(0, 4)], ao_r.at[o, 1])

    def act_done(r):
        wait_for(af.at[r, :, pl.ds(0, 4)], ag_r.at[r, 4])

    def act_sent(r):
        for k in range(4):
            @pl.when(jnp.logical_not(jnp.logical_and(same, y == k)))
            def _():
                wait_for(af.at[r, 0, 0, 0], a1_s.at[r, k])
        if r == 0:
            for o in range(4):
                wait_for(af.at[0, pl.ds(0, 3), pl.ds(0, 5), 0], ao_s.at[o, 0])
                wait_for(af.at[0, 0, pl.ds(0, 4)], ao_s.at[o, 1])
            return
        wait_for(af.at[r, pl.ds(0, 2), 0, pl.ds(0, 3)], ag_s.at[r, 0])
        wait_for(af.at[r, pl.ds(0, 2), 0, pl.ds(0, 3)], ag_s.at[r, 1])
        wait_for(af.at[r, pl.ds(0, 2), pl.ds(0, 3)], ag_s.at[r, 2])
        wait_for(af.at[r, pl.ds(0, 2), pl.ds(0, 3)], ag_s.at[r, 3])
        wait_for(af.at[r, :, pl.ds(0, 4)], ag_s.at[r, 4])

    def direct_tile(r, j):
        send(xn.at[r, 0, j, 1], rn.at[r, 0, j, 1], xn_s.at[r], xn_r.at[r, 0], (xp, t))
        send(xn.at[r, 1, j, 0], rn.at[r, 1, j, 0], xn_s.at[r], xn_r.at[r, 1], (xm, t))

    def far_tile(r, j, far):
        xo[r, j, 0] = far[:HB]
        xo[r, j, 1] = far[HB:]
        send(xo.at[r, j, 0], ro.at[r, 0, j], xo_s.at[r], xo_r.at[r, 0, j], (xp, t))
        send(xo.at[r, j, 1], ro.at[r, 1, j], xo_s.at[r], xo_r.at[r, 1, j], (xm, t))

    def multiply_far(r, start, stop):
        def step(j, carry):
            a = jnp.concatenate([af[r, (x + 2) % 4, b].reshape(RB, 256) for b in range(8)], axis=1)
            far_tile(r, j, jnp.dot(a, wv[j].reshape(2048, 256), preferred_element_type=F32).astype(BF))
            return carry

        lax.fori_loop(start, stop, step, 0)

    def multiply(r, at_once):
        def step(j, carry):
            w = wv[j].reshape(2048, 256)
            a = jnp.concatenate([af[r, :, b].reshape(4 * RB, 256) for b in range(8)], axis=1)
            pacc[...] = jnp.dot(a, w, preferred_element_type=F32).reshape(4, RB, 256)
            if r > 0:
                far_tile(r, j, pacc[(x + 2) % 4].astype(BF))
            nxt = pacc[xp]
            nb[r, 0, j] = nxt[:HB]
            xn[r, 0, j, 1] = nxt[HB:].astype(BF)
            prv = pacc[xm]
            nb[r, 1, j] = prv[HB:]
            xn[r, 1, j, 0] = prv[:HB].astype(BF)
            if at_once:
                direct_tile(r, j)
            own[r, j] = pacc[x]
            return carry

        lax.fori_loop(0, TILES, step, 0)

    def direct(r):
        def step(j, carry):
            direct_tile(r, j)
            return carry

        lax.fori_loop(0, TILES, step, 0)

    def relay(r):
        def step(j, carry):
            wait_for(ro.at[r, 0, j], xo_r.at[r, 0, j])
            xn[r, 0, j, 0] = (nb[r, 0, j] + ro[r, 0, j].astype(F32)).astype(BF)
            send(xn.at[r, 0, j, 0], rn.at[r, 0, j, 0], xn_s.at[r], xn_r.at[r, 0], (xp, t))
            wait_for(ro.at[r, 1, j], xo_r.at[r, 1, j])
            xn[r, 1, j, 1] = (nb[r, 1, j] + ro[r, 1, j].astype(F32)).astype(BF)
            send(xn.at[r, 1, j, 1], rn.at[r, 1, j, 1], xn_s.at[r], xn_r.at[r, 1], (xm, t))
            return carry

        lax.fori_loop(0, TILES, step, 0)

    def reduce_sent(r):
        wait_for(xo.at[r], xo_s.at[r])
        wait_for(xn.at[r], xn_s.at[r])

    def pieces(ref, k, count):
        return ref.at[k, pl.ds(0, count * PK[k])]

    def piece_of(k, q):
        return pl.ds(pl.multiple_of(q * PK[k], PK[k]), PK[k])

    def hide(r):
        k = PART_OF[r]
        count = RB // PIECE[k]
        first = (r - PARTS[k][0]) * count
        wait_for(rn.at[r, 0], xn_r.at[r, 0])
        wait_for(rn.at[r, 1], xn_r.at[r, 1])
        groups = []
        for j in range(TILES):
            s = own[r, j] + rn[r, 0, j].reshape(RB, 256).astype(F32) + rn[r, 1, j].reshape(RB, 256).astype(F32)
            g, u = s[:, :128], s[:, 128:]
            groups.append(g / (1.0 + jnp.exp(-g)) * u)
        hs[k, pl.ds(first * PK[k], count * PK[k])] = pack(groups, PIECE[k]).reshape(count * PK[k], 128)
        mine = piece_of(k, p)

        def step(i, carry):
            q = first + (p + i) % count

            @pl.when(q != p)
            def _():
                send(hs.at[k, piece_of(k, q)], hr.at[k, c, mine], h_s.at[k, 0], h_r.at[k, 0], (x, q * 2 + c))

            @pl.when(q == p)
            def _():
                hr[k, c, mine] = hs[k, mine]

            return carry

        lax.fori_loop(0, count, step, 0)

    def hide_sib(k):
        wait_for(pieces(hs, k, 15), h_r.at[k, 0])
        both = hr.at[k, c, pl.ds(0, 16 * PK[k])]
        send(both, both, h_s.at[k, 1], h_r.at[k, 1], at(x, y, z, sib))

    def mix(k):
        n, piece, every, mine = ROWS[k], PIECE[k], pl.ds(0, 16 * PK[k]), piece_of(k, p)
        wait_for(pieces(hs, k, 16), h_r.at[k, 1])
        both = jnp.concatenate([unpack(hr[k, i, every].reshape(16, PK[k], 128), piece) for i in range(2)], axis=0)
        mixed = jnp.dot(both, mhi[...], preferred_element_type=F32)
        mixed = mixed + jnp.dot(both, mlo[...], preferred_element_type=F32)
        sign = jnp.where(c == 0, 1.0, -1.0).astype(F32)
        s = mixed[:n] + sign * mixed[n:]
        if piece == 4:
            v = s.reshape(8, 8, SPAN)
            turned = jnp.concatenate([v[:, 4:], v[:, :4]], axis=1)
            low = lax.broadcasted_iota(jnp.int32, v.shape, 1) < 4
            s = jnp.where(low, v + turned, turned - v).reshape(n, SPAN)
        parts = [s[8 * i : 8 * i + 8] for i in range(n // 8)]
        half = 1
        while half < len(parts):
            for i in range(len(parts)):
                if i & half == 0:
                    a, b = parts[i], parts[i + half]
                    parts[i], parts[i + half] = a + b, a - b
            half *= 2
        for i in range(len(parts)):
            groups = [parts[i][:, 128 * g : 128 * g + 128] for g in range(TILES)]
            rs[k, pl.ds(i * 64, 64)] = pack(groups, piece).reshape(64, 128)
        rr[k, mine] = rs[k, mine]

        def step(i, carry):
            q = (p + i) % 16
            send(rs.at[k, piece_of(k, q)], rr.at[k, mine], h_s.at[k, 2], h_r.at[k, 2], (x, q * 2 + c))
            return carry

        lax.fori_loop(1, 16, step, 0)

    def mix_sent(k):
        wait_for(pieces(hs, k, 15), h_s.at[k, 0])
        wait_for(pieces(hs, k, 16), h_s.at[k, 1])
        wait_for(pieces(hs, k, 15), h_s.at[k, 2])

    def spread(k, i):
        h, rows, halves, top = ROWS[k] // 2, pl.ds(OFF[k], ROWS[k]), pl.ds(OFF[k] // 2, ROWS[k] // 2), pl.ds(0, ROWS[k])
        q = block(i)
        qy, qz = q // 4, q % 4
        wait_for(dr.at[q, rows], ds_r.at[k, q])
        e = (dk[q, top] + dr[q, rows].astype(F32)).astype(BF)
        if k == LAST:
            ed[q] = e

            @pl.when(i < 15)
            def _():
                send(ed.at[q], fd.at[p], e_s.at[k, 0], e_r.at[k, 0], (x, q * 2 + c))

            return
        es[0, qy, qz, halves] = e[:h]
        es[1, qy, qz, halves] = e[h:]

        @pl.when(qz != z)
        def _():
            slot = (qz + 3 - z) % 4
            dst = f1.at[0, slot, qy, halves]
            send(es.at[0, qy, qz, halves], dst, e_s.at[k, 0], e_r.at[k, 0], at(x, y, qz, c))

        @pl.when(qy != y)
        def _():
            slot = (qy + 3 - y) % 4
            dst = f1.at[1, slot, qz, halves]
            send(es.at[1, qy, qz, halves], dst, e_s.at[k, 1], e_r.at[k, 1], at(x, qy, z, c))

    def project(k, start, stop):
        rows, top = pl.ds(OFF[k], ROWS[k]), pl.ds(0, ROWS[k])
        if start == 0:
            wait_for(pieces(rr, k, 15), h_r.at[k, 2])
            rot[top, :] = unpack(rr[k, pl.ds(0, 16 * PK[k])].reshape(16, PK[k], 128), PIECE[k])

        def step(i, carry):
            q = block(i)
            d = jnp.dot(rot[top, :], dv[q], preferred_element_type=F32)
            left, right = d[:, :256], d[:, 256:]
            dk[q, top] = jnp.where(c == 0, left, right)
            ds[q, rows] = jnp.where(c == 0, right, left).astype(BF)
            send(ds.at[q, rows], dr.at[q, rows], ds_s.at[k], ds_r.at[k, q], at(x, y, z, sib))

            @pl.when(i >= LAG)
            def _():
                spread(k, i - LAG)

            return carry

        lax.fori_loop(start, stop, step, 0)

    def flush(k):
        def step(i, carry):
            spread(k, i)
            return carry

        lax.fori_loop(16 - LAG, 16, step, 0)

    def gather_one(k):
        halves = pl.ds(OFF[k] // 2, ROWS[k] // 2)
        for a in range(2):
            wait_for(f1.at[a, :, :, halves], e_r.at[k, a])
            total = es[0, :, z, halves].astype(F32) if a == 0 else es[1, y, :, halves].astype(F32)
            for i in range(3):
                total = total + f1[a, i, :, halves].astype(F32)
            g2[a, :, halves] = total.astype(BF)
            for i in range(1, 4):
                q = (y + i) % 4 if a == 0 else (z + i) % 4
                dev = at(x, q, z, c) if a == 0 else at(x, y, q, c)
                send(g2.at[a, q, halves], f2.at[a, i - 1, halves], e_s.at[k, 2 + a], e_r.at[k, 2 + a], dev)

    def finish(k):
        h = ROWS[k] // 2
        if k == LAST:
            wait_for(ed.at[pl.ds(0, 15)], e_r.at[k, 0])
            fd[p] = ed[p]
            total = fd[0].astype(F32)
            for i in range(1, 16):
                total = total + fd[i].astype(F32)
            out[pl.ds(OFF[k], ROWS[k]), :] = total.astype(BF)
            return
        halves = pl.ds(OFF[k] // 2, h)
        for a, own_block in ((0, y), (1, z)):
            wait_for(f2.at[a, :, halves], e_r.at[k, 2 + a])
            total = g2[a, own_block, halves].astype(F32)
            for i in range(3):
                total = total + f2[a, i, halves].astype(F32)
            out[pl.ds(OFF[k] + a * h, h), :] = total.astype(BF)

    def project_sent(k):
        halves = pl.ds(OFF[k] // 2, ROWS[k] // 2)
        wait_for(ds.at[:, pl.ds(OFF[k], ROWS[k])], ds_s.at[k])
        if k == LAST:
            wait_for(ed.at[pl.ds(0, 15)], e_s.at[k, 0])
            return
        for a in range(2):
            wait_for(f1.at[a, :, :, halves], e_s.at[k, a])
            wait_for(f2.at[a, :, halves], e_s.at[k, 2 + a])

    for r in range(CHUNKS):
        act_first(r)

    def build(i, carry):
        f_in = i * 128 + lax.broadcasted_iota(jnp.int32, (128, SPAN), 0)
        f_out = lax.broadcasted_iota(jnp.int32, (128, SPAN), 1)
        b_in, b_out = (f_in * 9363) >> 16, (f_out * 9363) >> 16
        a_in, a_out = f_in - 7 * b_in, f_out - 7 * b_out
        v = b_in & b_out
        v = v ^ (v >> 4)
        v = v ^ (v >> 2)
        v = v ^ (v >> 1)
        sign = (1 - 2 * (v & 1)).astype(F32)
        value = jnp.zeros((128, SPAN), F32)
        a_row = a_out[:8]
        for k in range(7):
            row = jnp.zeros((8, SPAN), F32)
            for m in range(7):
                row = jnp.where(a_row == m, gm[m, k], row)
            value = jnp.where(a_in == k, row[:1], value)
        value = value * sign * (1.0 / 64.0)
        hi = value.astype(BF)
        rows = pl.ds(pl.multiple_of(i * 128, 128), 128)
        mhi[rows, :] = hi
        mlo[rows, :] = (value - hi.astype(F32)).astype(BF)
        return carry

    lax.fori_loop(0, TILES, build, 0)

    own0_first(2)
    own0_a(2)
    own0_first(1)
    own0_a(1)
    own0_first(3)
    own0_a(3)
    own0_first(0)
    own0_a(0)
    act_first_done(1)
    act_a(1)
    act_first_done(2)
    act_a(2)
    act_first_done(3)
    act_a(3)
    wait_for(wv, w_sem)
    own0_sib(2)
    own0_sib(1)
    own0_sib(3)
    act_b(1)
    own0_done(2)
    multiply_far(0, 0, 3)
    own0_sib(0)
    act_b(2)
    multiply_far(0, 3, 7)
    act_b(3)
    own0_done(1)
    own0_done(3)
    own0_done(0)
    multiply(0, True)
    act_sib(1)
    relay(0)
    act_sib(2)
    act_done(1)
    multiply(1, True)
    act_sib(3)
    act_done(2)
    multiply(2, False)
    relay(1)
    direct(2)
    hide(0)
    act_done(3)
    multiply(3, False)
    down_start()
    relay(2)
    direct(3)
    hide(1)
    relay(3)
    hide_sib(0)
    mix(0)
    hide(2)
    hide(3)
    hide_sib(1)
    mix(1)
    wait_for(dv, d_sem)
    project(0, 0, 8)
    hide_sib(2)
    project(0, 8, 12)
    mix(2)
    project(0, 12, 16)
    project(1, 0, 4)
    flush(0)
    project(1, 4, 16)
    gather_one(0)
    project(2, 0, 4)
    flush(1)
    project(2, 4, 16)
    flush(2)
    finish(0)
    gather_one(1)
    finish(1)
    finish(2)
    for r in range(CHUNKS):
        act_sent(r)
        reduce_sent(r)
    for r in range(len(PARTS)):
        mix_sent(r)
        project_sent(r)


def local(activations, gate_weight, up_weight, group_mix, down_weight):
    any_space = pl.BlockSpec(memory_space=pl.ANY)
    dma = pltpu.SemaphoreType.DMA
    vm = pltpu.VMEM
    r, n = CHUNKS, len(PARTS)
    scratch = [
        vm((TILES, 2, 4, 256, 256), BF),
        vm((16, SPAN, 512), BF),
        vm((r, 4, 8, 4, Q, 256), BF),
        vm((4, RB, 256), F32),
        vm((r, TILES, RB, 256), F32),
        vm((r, 2, TILES, HB, 256), F32),
        vm((r, TILES, 2, HB, 256), BF),
        vm((r, 2, TILES, 2, HB, 256), BF),
        vm((r, 2, TILES, HB, 256), BF),
        vm((r, 2, TILES, 2, HB, 256), BF),
        vm((SPAN, SPAN), BF),
        vm((SPAN, SPAN), BF),
        vm((n, 16 * 64, 128), BF),
        vm((n, 2, 16 * 64, 128), BF),
        vm((n, 16 * 64, 128), BF),
        vm((n, 16 * 64, 128), BF),
        vm((128, SPAN), BF),
        vm((16, 256, 256), BF),
        vm((16, 128, 256), F32),
        vm((16, 256, 256), BF),
        vm((2, 4, 4, 128, 256), BF),
        vm((2, 3, 4, 128, 256), BF),
        vm((2, 4, 128, 256), BF),
        vm((2, 3, 128, 256), BF),
        vm((16, ROWS[-1], 256), BF),
        vm((16, ROWS[-1], 256), BF),
        dma(()), dma(()),
        dma((r, 4)), dma((r,)),
        dma((r, 5)), dma((r, 5)),
        dma((r,)), dma((r, 2, TILES)),
        dma((r,)), dma((r, 2)),
        dma((n, 3)), dma((n, 3)),
        dma((n,)), dma((n, 16)),
        dma((n, 4)), dma((n, 4)),
        dma((4,)), dma((4, 2)), dma((4, 2)),
    ]
    return pl.pallas_call(
        kernel,
        out_shape=jax.ShapeDtypeStruct((256, 256), BF),
        in_specs=[any_space, any_space, any_space, pl.BlockSpec(memory_space=pltpu.SMEM), any_space],
        out_specs=pl.BlockSpec(memory_space=pltpu.VMEM),
        scratch_shapes=scratch,
        compiler_params=pltpu.CompilerParams(
            collective_id=0, has_side_effects=True, vmem_limit_bytes=60 * 1024 * 1024
        ),
        cost_estimate=pl.CostEstimate(flops=12_000_000_000, bytes_accessed=24_000_000, transcendentals=230_000),
        name="ffn",
    )(
        activations,
        gate_weight.reshape(4, 2, 256, SPAN),
        up_weight.reshape(4, 2, 256, SPAN),
        group_mix,
        down_weight,
    )


def solution(mesh):
    return jax.shard_map(
        local,
        mesh=mesh,
        in_specs=(P("dp", "tensor"), P("dp", "tensor"), P("dp", "tensor"), P(), P("tensor", None)),
        out_specs=P("dp", "tensor"),
        check_vma=False,
    )
```

```python
import jax
import jax.numpy as jnp
from jax import lax
from jax.experimental import pallas as pl
from jax.experimental.pallas import tpu as pltpu
from jax.sharding import PartitionSpec as P

MESH = pl.DeviceIdType.MESH
BF = jnp.bfloat16
F32 = jnp.float32

CHUNKS = 4
RB = 256 // CHUNKS
PARTS = ((0, 1), (2,), (3,))
PART_OF = [k for k, part in enumerate(PARTS) for _ in part]
ROWS = [RB * len(part) for part in PARTS]
OFF = [RB * part[0] for part in PARTS]
LAST = len(PARTS) - 1
PIECE = [rows // 16 for rows in ROWS]
PK = [8 * piece for piece in PIECE]
Q = RB // 4
HB = RB // 2
TILES = 7
SPAN = 896
LAG = 4
GROUPS = 8


def wait_for(ref, sem):
    pltpu.make_async_copy(ref, ref, sem).wait()


def cross(a, b):
    low = lax.broadcasted_iota(jnp.int32, a.shape, a.ndim - 2) < 4
    half_turn = lambda v: jnp.concatenate([v[..., 4:, :], v[..., :4, :]], axis=-2)
    return jnp.where(low, a, half_turn(b)), jnp.where(low, half_turn(a), b)


def pack(groups, piece):
    rows = groups[0].shape[0]
    groups = [g.reshape(rows // 8, 8, 128) for g in groups]
    groups.append(jnp.zeros_like(groups[0]))
    if piece == 8:
        pairs = [jnp.concatenate(groups[i : i + 2], axis=1) for i in range(0, GROUPS, 2)]
        return jnp.concatenate([v.astype(BF) for v in pairs], axis=1)
    even, odd = zip(*[cross(groups[i], groups[i + 1]) for i in range(0, GROUPS, 2)])
    both = jnp.stack([jnp.concatenate(even, axis=1), jnp.concatenate(odd, axis=1)], axis=1)
    return both.reshape(rows // 4, 32, 128).astype(BF)


def unpack(packed, piece):
    out = []
    if piece == 8:
        for i in range(0, GROUPS, 2):
            pair = packed[:, i * 8 : i * 8 + 16, :].astype(F32)
            out += [pair[:, :8, :].reshape(128, 128), pair[:, 8:, :].reshape(128, 128)]
    else:
        both = packed.astype(F32).reshape(8, 2, 32, 128)
        for i in range(0, GROUPS, 2):
            rows = slice(4 * i, 4 * i + 8)
            first, second = cross(both[:, 0, rows], both[:, 1, rows])
            out += [first.reshape(64, 128), second.reshape(64, 128)]
    return jnp.concatenate([v.astype(BF) for v in out[:TILES]], axis=1)


def kernel(
    act, gate, up, gm, down, out,
    wv, dv, af, pacc, own, nb, xo, xn, ro, rn,
    mhi, mlo, hs, hr, rs, rr, rot, ds, dk, dr, es, f1, g2, f2, ed, fd,
    w_sem, d_sem, a1_s, a1_r, ag_s, ag_r, xo_s, xo_r, xn_s, xn_r,
    h_s, h_r, ds_s, ds_r, e_s, e_r, a0_r, ao_s, ao_r,
):
    x = lax.axis_index("dp")
    t = lax.axis_index("tensor")
    y, z, c = t // 8, (t // 2) % 4, t % 2
    p = t // 2
    sib = 1 - c
    xp, xm = (x + 1) % 4, (x + 3) % 4
    kb, kbs = c * 4 + z, pl.ds(c * 4, 4)

    def at(x_, y_, z_, c_):
        return (x_, y_ * 8 + z_ * 2 + c_)

    def send(src, dst, ss, rs_, dev):
        pltpu.make_async_remote_copy(
            src_ref=src, dst_ref=dst, send_sem=ss, recv_sem=rs_, device_id=dev, device_id_type=MESH
        ).start()

    for j in range(TILES):
        for cc in range(2):
            cols = pl.ds(j * 128, 128)
            pltpu.make_async_copy(gate.at[:, cc, :, cols], wv.at[j, cc, :, :, pl.ds(0, 128)], w_sem).start()
            pltpu.make_async_copy(up.at[:, cc, :, cols], wv.at[j, cc, :, :, pl.ds(128, 128)], w_sem).start()
    bar = pltpu.get_barrier_semaphore()

    def greet(dev):
        pl.semaphore_signal(bar, inc=1, device_id=dev, device_id_type=MESH)

    same = x == y
    greet((xp, t))
    greet((xm, t))
    greet(at(x, y, z, sib))
    for k in range(4):
        @pl.when(jnp.logical_not(jnp.logical_and(same, y == k)))
        def _():
            greet(at(y, k, z, c))

        @pl.when(jnp.logical_not(jnp.logical_and(same, x == k)))
        def _():
            greet(at(k, x, z, c))


    def greet_plane(i, carry):
        greet((x, (p + i) % 16 * 2 + c))
        return carry

    lax.fori_loop(1, 16, greet_plane, 0)
    pl.semaphore_wait(bar, jnp.where(same, 24, 26))

    def down_start():
        for j in range(16):
            pltpu.make_async_copy(down.at[:, pl.ds(j * 512, 512)], dv.at[j], d_sem).start()

    def act_first(r):
        sem = a0_r.at[x] if r == 0 else a1_r.at[r]
        for k in range(4):
            src = act.at[pl.ds(r * RB + k * Q, Q), :]
            dst = af.at[r, x, kb, k]
            here = jnp.logical_and(same, y == k)

            @pl.when(here)
            def _():
                pltpu.make_async_copy(src, dst, sem).start()

            @pl.when(jnp.logical_not(here))
            def _():
                send(src, dst, a1_s.at[r, k], sem, at(y, k, z, c))

    def act_first_done(r):
        wait_for(af.at[r, :, 0, 0], a1_r.at[r])

    def act_a(r):
        for i in range(1, 4):
            piece = af.at[r, pl.ds(0, 2), kb, y]
            send(piece, piece, ag_s.at[r, 0], ag_r.at[r, 0], at(x, (y + i) % 4, z, c))
            piece = af.at[r, pl.ds(2, 2), kb, y]
            send(piece, piece, ag_s.at[r, 1], ag_r.at[r, 1], at(x, y, (z + i) % 4, c))

    def act_b(r):
        wait_for(af.at[r, pl.ds(0, 2), 0, pl.ds(0, 3)], ag_r.at[r, 0])
        for i in range(1, 4):
            piece = af.at[r, pl.ds(0, 2), kb]
            send(piece, piece, ag_s.at[r, 2], ag_r.at[r, 2], at(x, y, (z + i) % 4, c))
        wait_for(af.at[r, pl.ds(0, 2), 0, pl.ds(0, 3)], ag_r.at[r, 1])
        for i in range(1, 4):
            piece = af.at[r, pl.ds(2, 2), kbs, y]
            send(piece, piece, ag_s.at[r, 3], ag_r.at[r, 3], at(x, (y + i) % 4, z, c))

    def act_sib(r):
        wait_for(af.at[r, pl.ds(0, 2), pl.ds(0, 3)], ag_r.at[r, 2])
        wait_for(af.at[r, pl.ds(0, 2), pl.ds(0, 3)], ag_r.at[r, 3])
        piece = af.at[r, :, kbs]
        send(piece, piece, ag_s.at[r, 4], ag_r.at[r, 4], at(x, y, z, sib))

    def block(i):
        a, b = i // 4, i % 4
        dy, dz = (3 * a * a + 3 * a + 6) % 7 % 4, (3 * b * b + 3 * b + 6) % 7 % 4
        return ((y + dy) % 4) * 4 + (z + dz) % 4

    def own0_first(o):
        wait_for(af.at[0, 0, 0, 0], a0_r.at[(x + o) % 4])

    def own0_a(o):
        piece = af.at[0, (x + o) % 4, kb, y]

        def step(i, carry):
            send(piece, piece, ao_s.at[o, 0], ao_r.at[o, 0], (x, block(i) * 2 + c))
            return carry

        lax.fori_loop(0, 15, step, 0)

    def own0_sib(o):
        wait_for(af.at[0, pl.ds(0, 3), pl.ds(0, 5), 0], ao_r.at[o, 0])
        piece = af.at[0, (x + o) % 4, kbs]
        send(piece, piece, ao_s.at[o, 1], ao_r.at[o, 1], at(x, y, z, sib))

    def own0_done(o):
        wait_for(af.at[0, 0, pl.ds(0, 4)], ao_r.at[o, 1])

    def act_done(r):
        wait_for(af.at[r, :, pl.ds(0, 4)], ag_r.at[r, 4])

    def act_sent(r):
        for k in range(4):
            @pl.when(jnp.logical_not(jnp.logical_and(same, y == k)))
            def _():
                wait_for(af.at[r, 0, 0, 0], a1_s.at[r, k])
        if r == 0:
            for o in range(4):
                wait_for(af.at[0, pl.ds(0, 3), pl.ds(0, 5), 0], ao_s.at[o, 0])
                wait_for(af.at[0, 0, pl.ds(0, 4)], ao_s.at[o, 1])
            return
        wait_for(af.at[r, pl.ds(0, 2), 0, pl.ds(0, 3)], ag_s.at[r, 0])
        wait_for(af.at[r, pl.ds(0, 2), 0, pl.ds(0, 3)], ag_s.at[r, 1])
        wait_for(af.at[r, pl.ds(0, 2), pl.ds(0, 3)], ag_s.at[r, 2])
        wait_for(af.at[r, pl.ds(0, 2), pl.ds(0, 3)], ag_s.at[r, 3])
        wait_for(af.at[r, :, pl.ds(0, 4)], ag_s.at[r, 4])

    def direct_tile(r, j):
        send(xn.at[r, 0, j, 1], rn.at[r, 0, j, 1], xn_s.at[r], xn_r.at[r, 0], (xp, t))
        send(xn.at[r, 1, j, 0], rn.at[r, 1, j, 0], xn_s.at[r], xn_r.at[r, 1], (xm, t))

    def far_tile(r, j, far):
        xo[r, j, 0] = far[:HB]
        xo[r, j, 1] = far[HB:]
        send(xo.at[r, j, 0], ro.at[r, 0, j], xo_s.at[r], xo_r.at[r, 0, j], (xp, t))
        send(xo.at[r, j, 1], ro.at[r, 1, j], xo_s.at[r], xo_r.at[r, 1, j], (xm, t))

    def multiply_far(r, start, stop):
        def step(j, carry):
            a = jnp.concatenate([af[r, (x + 2) % 4, b].reshape(RB, 256) for b in range(8)], axis=1)
            far_tile(r, j, jnp.dot(a, wv[j].reshape(2048, 256), preferred_element_type=F32).astype(BF))
            return carry

        lax.fori_loop(start, stop, step, 0)

    def multiply(r, at_once):
        def step(j, carry):
            w = wv[j].reshape(2048, 256)
            a = jnp.concatenate([af[r, :, b].reshape(4 * RB, 256) for b in range(8)], axis=1)
            pacc[...] = jnp.dot(a, w, preferred_element_type=F32).reshape(4, RB, 256)
            if r > 0:
                far_tile(r, j, pacc[(x + 2) % 4].astype(BF))
            nxt = pacc[xp]
            nb[r, 0, j] = nxt[:HB]
            xn[r, 0, j, 1] = nxt[HB:].astype(BF)
            prv = pacc[xm]
            nb[r, 1, j] = prv[HB:]
            xn[r, 1, j, 0] = prv[:HB].astype(BF)
            if at_once:
                direct_tile(r, j)
            own[r, j] = pacc[x]
            return carry

        lax.fori_loop(0, TILES, step, 0)

    def direct(r):
        def step(j, carry):
            direct_tile(r, j)
            return carry

        lax.fori_loop(0, TILES, step, 0)

    def relay(r):
        def step(j, carry):
            wait_for(ro.at[r, 0, j], xo_r.at[r, 0, j])
            xn[r, 0, j, 0] = (nb[r, 0, j] + ro[r, 0, j].astype(F32)).astype(BF)
            send(xn.at[r, 0, j, 0], rn.at[r, 0, j, 0], xn_s.at[r], xn_r.at[r, 0], (xp, t))
            wait_for(ro.at[r, 1, j], xo_r.at[r, 1, j])
            xn[r, 1, j, 1] = (nb[r, 1, j] + ro[r, 1, j].astype(F32)).astype(BF)
            send(xn.at[r, 1, j, 1], rn.at[r, 1, j, 1], xn_s.at[r], xn_r.at[r, 1], (xm, t))
            return carry

        lax.fori_loop(0, TILES, step, 0)

    def reduce_sent(r):
        wait_for(xo.at[r], xo_s.at[r])
        wait_for(xn.at[r], xn_s.at[r])

    def pieces(ref, k, count):
        return ref.at[k, pl.ds(0, count * PK[k])]

    def piece_of(k, q):
        return pl.ds(pl.multiple_of(q * PK[k], PK[k]), PK[k])

    def hide(r):
        k = PART_OF[r]
        count = RB // PIECE[k]
        first = (r - PARTS[k][0]) * count
        wait_for(rn.at[r, 0], xn_r.at[r, 0])
        wait_for(rn.at[r, 1], xn_r.at[r, 1])
        groups = []
        for j in range(TILES):
            s = own[r, j] + rn[r, 0, j].reshape(RB, 256).astype(F32) + rn[r, 1, j].reshape(RB, 256).astype(F32)
            g, u = s[:, :128], s[:, 128:]
            groups.append(g / (1.0 + jnp.exp(-g)) * u)
        hs[k, pl.ds(first * PK[k], count * PK[k])] = pack(groups, PIECE[k]).reshape(count * PK[k], 128)
        mine = piece_of(k, p)

        def step(i, carry):
            q = first + (p + i) % count

            @pl.when(q != p)
            def _():
                send(hs.at[k, piece_of(k, q)], hr.at[k, c, mine], h_s.at[k, 0], h_r.at[k, 0], (x, q * 2 + c))

            @pl.when(q == p)
            def _():
                hr[k, c, mine] = hs[k, mine]

            return carry

        lax.fori_loop(0, count, step, 0)

    def hide_sib(k):
        wait_for(pieces(hs, k, 15), h_r.at[k, 0])
        both = hr.at[k, c, pl.ds(0, 16 * PK[k])]
        send(both, both, h_s.at[k, 1], h_r.at[k, 1], at(x, y, z, sib))

    def mix(k):
        n, piece, every, mine = ROWS[k], PIECE[k], pl.ds(0, 16 * PK[k]), piece_of(k, p)
        wait_for(pieces(hs, k, 16), h_r.at[k, 1])
        both = jnp.concatenate([unpack(hr[k, i, every].reshape(16, PK[k], 128), piece) for i in range(2)], axis=0)
        mixed = jnp.dot(both, mhi[...], preferred_element_type=F32)
        mixed = mixed + jnp.dot(both, mlo[...], preferred_element_type=F32)
        sign = jnp.where(c == 0, 1.0, -1.0).astype(F32)
        s = mixed[:n] + sign * mixed[n:]
        if piece == 4:
            v = s.reshape(8, 8, SPAN)
            turned = jnp.concatenate([v[:, 4:], v[:, :4]], axis=1)
            low = lax.broadcasted_iota(jnp.int32, v.shape, 1) < 4
            s = jnp.where(low, v + turned, turned - v).reshape(n, SPAN)
        parts = [s[8 * i : 8 * i + 8] for i in range(n // 8)]
        half = 1
        while half < len(parts):
            for i in range(len(parts)):
                if i & half == 0:
                    a, b = parts[i], parts[i + half]
                    parts[i], parts[i + half] = a + b, a - b
            half *= 2
        for i in range(len(parts)):
            groups = [parts[i][:, 128 * g : 128 * g + 128] for g in range(TILES)]
            rs[k, pl.ds(i * 64, 64)] = pack(groups, piece).reshape(64, 128)
        rr[k, mine] = rs[k, mine]

        def step(i, carry):
            q = (p + i) % 16
            send(rs.at[k, piece_of(k, q)], rr.at[k, mine], h_s.at[k, 2], h_r.at[k, 2], (x, q * 2 + c))
            return carry

        lax.fori_loop(1, 16, step, 0)

    def mix_sent(k):
        wait_for(pieces(hs, k, 15), h_s.at[k, 0])
        wait_for(pieces(hs, k, 16), h_s.at[k, 1])
        wait_for(pieces(hs, k, 15), h_s.at[k, 2])

    def spread(k, i):
        h, rows, halves, top = ROWS[k] // 2, pl.ds(OFF[k], ROWS[k]), pl.ds(OFF[k] // 2, ROWS[k] // 2), pl.ds(0, ROWS[k])
        q = block(i)
        qy, qz = q // 4, q % 4
        wait_for(dr.at[q, rows], ds_r.at[k, q])
        e = (dk[q, top] + dr[q, rows].astype(F32)).astype(BF)
        if k == LAST:
            ed[q] = e

            @pl.when(i < 15)
            def _():
                send(ed.at[q], fd.at[p], e_s.at[k, 0], e_r.at[k, 0], (x, q * 2 + c))

            return
        es[0, qy, qz, halves] = e[:h]
        es[1, qy, qz, halves] = e[h:]

        @pl.when(qz != z)
        def _():
            slot = (qz + 3 - z) % 4
            dst = f1.at[0, slot, qy, halves]
            send(es.at[0, qy, qz, halves], dst, e_s.at[k, 0], e_r.at[k, 0], at(x, y, qz, c))

        @pl.when(qy != y)
        def _():
            slot = (qy + 3 - y) % 4
            dst = f1.at[1, slot, qz, halves]
            send(es.at[1, qy, qz, halves], dst, e_s.at[k, 1], e_r.at[k, 1], at(x, qy, z, c))

    def project(k, start, stop):
        rows, top = pl.ds(OFF[k], ROWS[k]), pl.ds(0, ROWS[k])
        if start == 0:
            wait_for(pieces(rr, k, 15), h_r.at[k, 2])
            rot[top, :] = unpack(rr[k, pl.ds(0, 16 * PK[k])].reshape(16, PK[k], 128), PIECE[k])

        def step(i, carry):
            q = block(i)
            d = jnp.dot(rot[top, :], dv[q], preferred_element_type=F32)
            left, right = d[:, :256], d[:, 256:]
            dk[q, top] = jnp.where(c == 0, left, right)
            ds[q, rows] = jnp.where(c == 0, right, left).astype(BF)
            send(ds.at[q, rows], dr.at[q, rows], ds_s.at[k], ds_r.at[k, q], at(x, y, z, sib))

            @pl.when(i >= LAG)
            def _():
                spread(k, i - LAG)

            return carry

        lax.fori_loop(start, stop, step, 0)

    def flush(k):
        def step(i, carry):
            spread(k, i)
            return carry

        lax.fori_loop(16 - LAG, 16, step, 0)

    def gather_one(k):
        halves = pl.ds(OFF[k] // 2, ROWS[k] // 2)
        for a in range(2):
            wait_for(f1.at[a, :, :, halves], e_r.at[k, a])
            total = es[0, :, z, halves].astype(F32) if a == 0 else es[1, y, :, halves].astype(F32)
            for i in range(3):
                total = total + f1[a, i, :, halves].astype(F32)
            g2[a, :, halves] = total.astype(BF)
            for i in range(1, 4):
                q = (y + i) % 4 if a == 0 else (z + i) % 4
                dev = at(x, q, z, c) if a == 0 else at(x, y, q, c)
                send(g2.at[a, q, halves], f2.at[a, i - 1, halves], e_s.at[k, 2 + a], e_r.at[k, 2 + a], dev)

    def finish(k):
        h = ROWS[k] // 2
        if k == LAST:
            wait_for(ed.at[pl.ds(0, 15)], e_r.at[k, 0])
            fd[p] = ed[p]
            total = fd[0].astype(F32)
            for i in range(1, 16):
                total = total + fd[i].astype(F32)
            out[pl.ds(OFF[k], ROWS[k]), :] = total.astype(BF)
            return
        halves = pl.ds(OFF[k] // 2, h)
        for a, own_block in ((0, y), (1, z)):
            wait_for(f2.at[a, :, halves], e_r.at[k, 2 + a])
            total = g2[a, own_block, halves].astype(F32)
            for i in range(3):
                total = total + f2[a, i, halves].astype(F32)
            out[pl.ds(OFF[k] + a * h, h), :] = total.astype(BF)

    def project_sent(k):
        halves = pl.ds(OFF[k] // 2, ROWS[k] // 2)
        wait_for(ds.at[:, pl.ds(OFF[k], ROWS[k])], ds_s.at[k])
        if k == LAST:
            wait_for(ed.at[pl.ds(0, 15)], e_s.at[k, 0])
            return
        for a in range(2):
            wait_for(f1.at[a, :, :, halves], e_s.at[k, a])
            wait_for(f2.at[a, :, halves], e_s.at[k, 2 + a])

    for r in range(CHUNKS):
        act_first(r)

    def build(i, carry):
        f_in = i * 128 + lax.broadcasted_iota(jnp.int32, (128, SPAN), 0)
        f_out = lax.broadcasted_iota(jnp.int32, (128, SPAN), 1)
        b_in, b_out = (f_in * 9363) >> 16, (f_out * 9363) >> 16
        a_in, a_out = f_in - 7 * b_in, f_out - 7 * b_out
        v = b_in & b_out
        v = v ^ (v >> 4)
        v = v ^ (v >> 2)
        v = v ^ (v >> 1)
        sign = (1 - 2 * (v & 1)).astype(F32)
        value = jnp.zeros((128, SPAN), F32)
        a_row = a_out[:8]
        for k in range(7):
            row = jnp.zeros((8, SPAN), F32)
            for m in range(7):
                row = jnp.where(a_row == m, gm[m, k], row)
            value = jnp.where(a_in == k, row[:1], value)
        value = value * sign * (1.0 / 64.0)
        hi = value.astype(BF)
        rows = pl.ds(pl.multiple_of(i * 128, 128), 128)
        mhi[rows, :] = hi
        mlo[rows, :] = (value - hi.astype(F32)).astype(BF)
        return carry

    lax.fori_loop(0, TILES, build, 0)

    own0_first(2)
    own0_a(2)
    own0_first(1)
    own0_a(1)
    own0_first(3)
    own0_a(3)
    own0_first(0)
    own0_a(0)
    act_first_done(1)
    act_a(1)
    act_first_done(2)
    act_a(2)
    act_first_done(3)
    act_a(3)
    wait_for(wv, w_sem)
    own0_sib(2)
    own0_sib(1)
    own0_sib(3)
    act_b(1)
    own0_done(2)
    multiply_far(0, 0, 3)
    own0_sib(0)
    act_b(2)
    multiply_far(0, 3, 7)
    act_b(3)
    own0_done(1)
    own0_done(3)
    own0_done(0)
    multiply(0, True)
    act_sib(1)
    relay(0)
    act_sib(2)
    act_done(1)
    multiply(1, True)
    act_sib(3)
    act_done(2)
    multiply(2, False)
    relay(1)
    direct(2)
    hide(0)
    act_done(3)
    multiply(3, False)
    down_start()
    relay(2)
    direct(3)
    hide(1)
    relay(3)
    hide_sib(0)
    mix(0)
    hide(2)
    hide(3)
    hide_sib(1)
    mix(1)
    wait_for(dv, d_sem)
    project(0, 0, 8)
    hide_sib(2)
    project(0, 8, 12)
    mix(2)
    project(0, 12, 16)
    flush(0)
    project(1, 0, 16)
    gather_one(0)
    project(2, 0, 4)
    flush(1)
    project(2, 4, 16)
    flush(2)
    finish(0)
    gather_one(1)
    finish(1)
    finish(2)
    for r in range(CHUNKS):
        act_sent(r)
        reduce_sent(r)
    for r in range(len(PARTS)):
        mix_sent(r)
        project_sent(r)


def local(activations, gate_weight, up_weight, group_mix, down_weight):
    any_space = pl.BlockSpec(memory_space=pl.ANY)
    dma = pltpu.SemaphoreType.DMA
    vm = pltpu.VMEM
    r, n = CHUNKS, len(PARTS)
    scratch = [
        vm((TILES, 2, 4, 256, 256), BF),
        vm((16, SPAN, 512), BF),
        vm((r, 4, 8, 4, Q, 256), BF),
        vm((4, RB, 256), F32),
        vm((r, TILES, RB, 256), F32),
        vm((r, 2, TILES, HB, 256), F32),
        vm((r, TILES, 2, HB, 256), BF),
        vm((r, 2, TILES, 2, HB, 256), BF),
        vm((r, 2, TILES, HB, 256), BF),
        vm((r, 2, TILES, 2, HB, 256), BF),
        vm((SPAN, SPAN), BF),
        vm((SPAN, SPAN), BF),
        vm((n, 16 * 64, 128), BF),
        vm((n, 2, 16 * 64, 128), BF),
        vm((n, 16 * 64, 128), BF),
        vm((n, 16 * 64, 128), BF),
        vm((128, SPAN), BF),
        vm((16, 256, 256), BF),
        vm((16, 128, 256), F32),
        vm((16, 256, 256), BF),
        vm((2, 4, 4, 128, 256), BF),
        vm((2, 3, 4, 128, 256), BF),
        vm((2, 4, 128, 256), BF),
        vm((2, 3, 128, 256), BF),
        vm((16, ROWS[-1], 256), BF),
        vm((16, ROWS[-1], 256), BF),
        dma(()), dma(()),
        dma((r, 4)), dma((r,)),
        dma((r, 5)), dma((r, 5)),
        dma((r,)), dma((r, 2, TILES)),
        dma((r,)), dma((r, 2)),
        dma((n, 3)), dma((n, 3)),
        dma((n,)), dma((n, 16)),
        dma((n, 4)), dma((n, 4)),
        dma((4,)), dma((4, 2)), dma((4, 2)),
    ]
    return pl.pallas_call(
        kernel,
        out_shape=jax.ShapeDtypeStruct((256, 256), BF),
        in_specs=[any_space, any_space, any_space, pl.BlockSpec(memory_space=pltpu.SMEM), any_space],
        out_specs=pl.BlockSpec(memory_space=pltpu.VMEM),
        scratch_shapes=scratch,
        compiler_params=pltpu.CompilerParams(
            collective_id=0, has_side_effects=True, vmem_limit_bytes=60 * 1024 * 1024
        ),
        cost_estimate=pl.CostEstimate(flops=12_000_000_000, bytes_accessed=24_000_000, transcendentals=230_000),
        name="ffn",
    )(
        activations,
        gate_weight.reshape(4, 2, 256, SPAN),
        up_weight.reshape(4, 2, 256, SPAN),
        group_mix,
        down_weight,
    )


def solution(mesh):
    return jax.shard_map(
        local,
        mesh=mesh,
        in_specs=(P("dp", "tensor"), P("dp", "tensor"), P("dp", "tensor"), P(), P("tensor", None)),
        out_specs=P("dp", "tensor"),
        check_vma=False,
    )
```
